256 devices in a mesh: rows: 64 (over z, x, core), cls: 4 (over y).
Axes of the slice: x: 4, y: 4, z: 8, core: 2. Of those that a mesh axis runs over, the one named last changes fastest.
Arguments:
- seed_scores: float32 [1000, 65536], P('cls', 'rows'), may hold values from 0 to 1, as said below
- block_columns: int32 [512, 8], P('rows'), may hold values from 0 to 511, as said below
- affinity: bfloat16 [512, 8, 128, 128], P('rows'), as said below
Outputs:
- pseudo_labels: float32 [1000, 65536], P('cls', 'rows')
The draws below stay inside these ranges and needn't reach their ends.
Inputs may be any that keep to these rules, and one draw needn't show every extreme that they name: `block_columns`: block row r lists 8 different block columns, each within 4 block rows of r counted cyclically over the 512 block rows; if row r lists column c then row c lists column r. `affinity`: all values are positive, and the block of row r at column c is the transpose of the block of row c at column r, so A is symmetric. `seed_scores`: every node has at most one nonzero entry, which is positive; every class has at least one labelled node.
All inputs are finite; a program needn't handle non-finite values.
Results may differ from the reference program's by a relative error of at most 0.0034.
Values may be sent and summed in bfloat16 or wider, within the bound.
A program may use at most 64 MiB of HBM per device.

```python
import math
import jax
import jax.numpy as jnp
from jax import lax

CLASSES = 1000
BLK = 128
BAND = 4
NNZB = 8
ITERS = 3
NBR = 512
NODES = 65536


def band_offsets(key):
    key_phase, key_order = jax.random.split(jax.random.fold_in(key, 17))
    phase_shift = jax.random.randint(key_phase, (), 0, 2 * BAND)
    row_index = jnp.arange(NBR, dtype=jnp.int32)
    long_reach = jnp.where((row_index + phase_shift) // BAND % 2 == 0, BAND, -BAND).astype(jnp.int32)
    near_offsets = jnp.concatenate([jnp.arange(BAND, dtype=jnp.int32), -jnp.arange(1, BAND, dtype=jnp.int32)])
    offsets = jnp.concatenate([jnp.broadcast_to(near_offsets[None, :], (NBR, 2 * BAND - 1)), long_reach[:, None]], axis=1)
    scores = jax.random.randint(key_order, (NBR, NNZB), 0, 2 ** 20) * NNZB + jnp.arange(NNZB, dtype=jnp.int32)[None, :]
    ordering = jnp.argsort(scores, axis=1, stable=True)
    return jnp.take_along_axis(offsets, ordering, axis=1)


def draw_block_columns(key, part):
    offsets = band_offsets(key)
    row_index = jnp.arange(NBR, dtype=jnp.int32)
    return ((row_index[:, None] + offsets) % NBR).astype(jnp.int32)


def draw_affinity(key, part):
    offsets = band_offsets(key)
    key = jax.random.fold_in(key, 2)
    key_uniform = jax.random.fold_in(key, 0)
    key_self = jax.random.fold_in(key, 5)
    uniform = jnp.exp(jax.random.uniform(key_uniform, (NBR, BAND + 1, BLK, BLK), jnp.float32, math.log(0.001), 0.0))
    row_index = jnp.arange(NBR, dtype=jnp.int32)
    column_row = (row_index[:, None] + offsets) % NBR
    source_row = jnp.where(offsets >= 0, row_index[:, None], column_row)
    gathered = uniform[source_row, jnp.abs(offsets)]
    flipped = jnp.swapaxes(gathered, 2, 3)
    kinds = offsets[:, :, None, None]
    blocks = jnp.where(kinds == 0, 0.5 * (gathered + flipped), jnp.where(kinds > 0, gathered, flipped))
    self_weight = jnp.exp(jax.random.uniform(key_self, (NBR, BLK), jnp.float32, math.log(0.2), math.log(100.0)))
    identity = (jnp.arange(BLK, dtype=jnp.int32)[:, None] == jnp.arange(BLK, dtype=jnp.int32)[None, :]).astype(jnp.float32)
    own_block = (offsets == 0).astype(jnp.float32)[:, :, None, None]
    blocks = blocks + own_block * identity[None, None, :, :] * self_weight[:, None, :, None]
    return blocks.astype(jnp.bfloat16)


def draw_seed_scores(key, part):
    key = jax.random.fold_in(key, 3)
    key_base, key_pick, key_first, key_second, key_order, key_jitter = jax.random.split(key, 6)
    row_index = jnp.arange(NBR, dtype=jnp.int32)
    base_rate = jax.random.randint(key_base, (NBR,), 8, 65)
    row_rate = base_rate * (NBR + 2 * row_index) // NBR
    node_rate = jnp.repeat(row_rate, BLK, total_repeat_length=NODES)
    picked = jax.random.randint(key_pick, (NODES,), 0, 1024) < node_rate
    first_draw = jax.random.randint(key_first, (NODES,), 0, CLASSES)
    second_draw = jax.random.randint(key_second, (NODES,), 0, CLASSES)
    rank = first_draw * second_draw // CLASSES
    class_order = jax.random.permutation(key_order, jnp.arange(CLASSES, dtype=jnp.int32))
    random_class = class_order[rank]
    stride = NODES // CLASSES
    node_index = jnp.arange(NODES, dtype=jnp.int32)
    stride_index = node_index // stride
    jitter = jax.random.randint(key_jitter, (CLASSES,), 0, stride)
    forced = (stride_index < CLASSES) & (node_index - stride_index * stride == jitter[jnp.minimum(stride_index, CLASSES - 1)])
    label_class = jnp.where(forced, stride_index, random_class)
    labelled = forced | picked
    onehot = ((jnp.arange(CLASSES, dtype=jnp.int32)[:, None] == label_class[None, :]) & labelled[None, :]).astype(jnp.float32)
    return onehot


def setup_inputs(seed: int = 0) -> dict:
    key_of = jax.random.split(jax.random.key(seed), 4)
    seed_scores = draw_seed_scores(jax.random.fold_in(key_of[3], 71), 0)
    block_columns = draw_block_columns(jax.random.fold_in(key_of[3], 71), 0)
    affinity = draw_affinity(jax.random.fold_in(key_of[3], 71), 0)
    return dict(seed_scores=seed_scores, block_columns=block_columns, affinity=affinity)


damping = 0.99
epsilon = 1e-06

def degree_scale(affinity):
    degree = lax.optimization_barrier(jnp.sum(affinity.astype(jnp.float32), axis=(1, 3)))
    return lax.rsqrt(degree).reshape(-1)

def propagate_once(direction, inverse_root, affinity, block_columns):
    scaled = (direction * inverse_root[None, :]).astype(jnp.bfloat16)
    blocks = scaled.reshape(CLASSES, NBR, BLK)
    summed = jnp.zeros((CLASSES, NBR, BLK), jnp.float32)
    for entry_index in range(NNZB):
        picked = blocks[:, block_columns[:, entry_index], :].astype(jnp.float32)
        values = affinity[:, entry_index].astype(jnp.float32)
        summed = summed + jnp.einsum('rab,crb->cra', values, picked)
    return direction - damping * inverse_root[None, :] * summed.reshape(CLASSES, NODES)

def reference(seed_scores, block_columns, affinity):
    inverse_root = degree_scale(affinity)
    solution = jnp.zeros_like(seed_scores)
    residual = seed_scores
    direction = seed_scores
    norm_now = lax.optimization_barrier(jnp.sum(residual * residual, axis=1, keepdims=True))
    for iteration in range(ITERS):
        mapped = propagate_once(direction, inverse_root, affinity, block_columns)
        step_size = norm_now / lax.optimization_barrier(jnp.sum(direction * mapped, axis=1, keepdims=True))
        solution = solution + step_size * direction
        residual = residual - step_size * mapped
        norm_next = lax.optimization_barrier(jnp.sum(residual * residual, axis=1, keepdims=True))
        direction = residual + norm_next / norm_now * direction
        norm_now = norm_next
    strength = lax.optimization_barrier(jnp.sum(solution * solution, axis=0, keepdims=True))
    return solution * lax.rsqrt(strength + epsilon)
```

```python
import functools

import jax
import jax.numpy as jnp
from jax import lax
from jax.experimental import pallas as pl
from jax.experimental.pallas import tpu as pltpu
from jax.sharding import PartitionSpec as P

MESH = pl.DeviceIdType.MESH
BAND = 4
NNZB = 8
BLK = 128
WIDE = 256
GROUP = 8
VMEM_BYTES = 527 * 1024 * 1024 // 10
damping = 0.99
epsilon = 1e-06
F32 = jnp.float32
BF16 = jnp.bfloat16


def column(table, index, width):
    return jnp.broadcast_to(table[:, index : index + 1], (BLK, width))


def node_sum(x):
    return jnp.sum(x, axis=0, keepdims=True)


def ratio(top, bottom):
    good = (bottom > 0) & (top > 0)
    return jnp.where(good, top / jnp.where(good, bottom, 1.0), 0.0)


def combination(early, middle, q):
    g00, g01, g11 = early
    g02, g12, g22 = middle
    g = damping
    gram = [[g00, g01, g02, g12], [g01, g11, g12, g22], [g02, g12, g22, q]]

    def square(p):
        return sum(p[i] * p[j] * gram[i][j] for i in range(len(p)) for j in range(len(p)))

    def energy(p):
        return sum(
            p[i] * p[j] * (gram[i][j] - g * gram[i][j + 1])
            for i in range(len(p))
            for j in range(len(p))
        )

    a0 = ratio(g00, g00 - g * g01)
    r1 = [1.0 - a0, g * a0]
    rr1 = square(r1)
    b0 = ratio(rr1, g00)
    d1 = [r1[0] + b0, r1[1]]
    a1 = ratio(rr1, energy(d1))
    r2 = [r1[0] - a1 * d1[0], r1[1] - a1 * (d1[1] - g * d1[0]), a1 * g * d1[1]]
    rr2 = square(r2)
    b1 = ratio(rr2, rr1)
    d2 = [r2[0] + b1 * d1[0], r2[1] + b1 * d1[1], r2[2]]
    a2 = ratio(rr2, energy(d2))
    return a0 + a1 * d1[0] + a2 * d2[0], a1 * d1[1] + a2 * d2[1], a2 * d2[2]


OWN = {i: (max(i, 2), min(i + 4, 5)) for i in range(4)}
HALO = {0: (0, 1), 1: (1, 1), 2: (6, 6), 3: (6, 7)}
OUTER = (0, 1, 6, 7)
TILES = ((0, 0), (0, 1), (1, 1), (2, 6), (3, 6), (3, 7))


def kernel(
    n_rows, n_cls,
    seed_hbm, columns_hbm, affinity_hbm, result,
    columns_ref, seed, raw, band, across, field1, field2a, field2b, field3a, field3b, v0, v1, v2, root, self_part, outer_root, outer_v0, outer_self,
    reach, turned1, turned2,
    code_out, code_left, code_right, apart_out, apart_left, apart_right, first_out, first_in, second_out, second_in,
    part_a, part_b, part_all, got_a, got_b, got_all, strength_out, strength_in,
    load_sem, halo_send, halo_recv, sum_send, sum_recv, cls_send, cls_recv, relay_sem,
):
    me = lax.axis_index("rows")
    mine = lax.axis_index("cls")
    low, high = lax.rem(me, GROUP), me // GROUP
    n_high = n_rows // GROUP
    total_blocks = n_rows * 8

    columns_copy = pltpu.make_async_copy(columns_hbm, columns_ref, load_sem.at[9])
    columns_copy.start()
    seed_copy = pltpu.make_async_copy(seed_hbm, seed, load_sem.at[8])
    seed_copy.start()
    raw_copies = []
    for r in range(8):
        copy = pltpu.make_async_copy(affinity_hbm.at[r], raw.at[r], load_sem.at[r])
        copy.start()
        raw_copies.append(copy)

    left = {"rows": lax.rem(me + n_rows - 1, n_rows), "cls": mine}
    right = {"rows": lax.rem(me + 1, n_rows), "cls": mine}
    far = sorted(range(1, GROUP), key=lambda d: -min(d, GROUP - d))
    peers_a = [{"rows": high * GROUP + lax.rem(low + d, GROUP), "cls": mine} for d in far]
    far = sorted(range(1, n_high), key=lambda d: -min(d, n_high - d))
    peers_b = [{"rows": lax.rem(high + d, n_high) * GROUP + low, "cls": mine} for d in far]
    far = sorted(range(1, n_cls), key=lambda d: -min(d, n_cls - d))
    peers_c = [{"rows": me, "cls": lax.rem(mine + d, n_cls)} for d in far]
    barrier = pltpu.get_barrier_semaphore()
    above = {"rows": lax.rem(high + 1, n_high) * GROUP + low, "cls": mine}
    below = {"rows": lax.rem(high + n_high - 1, n_high) * GROUP + low, "cls": mine}
    later = list(range(1, n_high)) + [0]
    peers_all = [
        {"rows": lax.rem(high + dz, n_high) * GROUP + lax.rem(low + d, GROUP), "cls": mine}
        for dz in later
        for d in range(GROUP)
        if (dz, d) != (0, 0)
    ]
    partners = [left, right] + [above, below] + peers_a + peers_c
    for device in partners:
        pl.semaphore_signal(barrier, inc=1, device_id=device, device_id_type=MESH)

    sent = []

    def send(source, target, send_sem, recv_sem, device):
        copy = pltpu.make_async_remote_copy(
            src_ref=source, dst_ref=target, send_sem=send_sem, recv_sem=recv_sem,
            device_id=device, device_id_type=MESH,
        )
        copy.start()
        sent.append(copy)
        return copy

    def packed(sums):
        pieces = [half for x in sums for half in (x[:, :BLK], x[:, BLK:])]
        if len(pieces) < 8:
            pieces.append(jnp.zeros((8 - len(pieces), BLK), F32))
        return jnp.concatenate(pieces, axis=0)

    def scatter(tile, out, got, peers, send_sem, recv_sem):
        out[...] = tile
        for d, device in enumerate(peers):
            copy = pltpu.make_async_remote_copy(
                src_ref=out, dst_ref=got.at[d], send_sem=send_sem, recv_sem=recv_sem,
                device_id=device, device_id_type=MESH,
            )
            copy.start()
        if peers:
            scattered.append((got, send_sem))
        return tile, got, peers, recv_sem

    def gather(tile, got, peers, recv_sem):
        if peers:
            pltpu.make_async_copy(got, got, recv_sem).wait()
            tile = tile + jnp.sum(got[...], axis=0)
        return tile

    scattered = []

    n_relays = n_high // 2

    def relay(step):
        if 0 < step <= n_relays:
            pl.semaphore_wait(relay_sem.at[step - 1], 2)
        if step < n_relays:
            for device in (above, below):
                pl.semaphore_signal(relay_sem.at[step], inc=1, device_id=device, device_id_type=MESH)

    lane = lax.broadcasted_iota(jnp.int32, (BLK, BLK), 1)
    diagonal = lane == lax.broadcasted_iota(jnp.int32, (BLK, BLK), 0)
    wide_lane = lax.broadcasted_iota(jnp.int32, (BLK, WIDE), 1).astype(F32)
    columns_copy.wait()
    places = []
    for r in range(8):
        offsets = [
            lax.rem(columns_ref[r, j] - (me * 8 + r) + BAND + total_blocks, total_blocks) for j in range(NNZB)
        ]
        absent = sum(range(9)) - sum(offsets)
        slots = []
        for o in range(9):
            j = 0
            for i in range(1, NNZB):
                j = jnp.where(offsets[i] == o, i, j)
            slots.append((j, (absent != o).astype(F32)))
        places.append(slots)

    seed_copy.wait()
    scores = seed[...]
    class_id = lax.broadcasted_iota(jnp.int32, scores.shape, 0).astype(F32)
    value = node_sum(scores)
    label = node_sum(jnp.where(scores > 0, class_id, 0.0))
    rows = [value[:, BLK * r : BLK * (r + 1)] for r in range(8)]
    rows += [label[:, BLK * r : BLK * (r + 1)] for r in range(8)]
    rows = jnp.concatenate(rows, axis=0)
    code_out[:16] = rows
    code = jnp.concatenate([rows, jnp.zeros((BLK - 16, BLK), F32)], axis=0).T
    for r in range(8):
        v0[BLK * r : BLK * (r + 1)] = jnp.where(
            column(code, 8 + r, WIDE) == wide_lane, column(code, r, WIDE), 0.0
        )

    inverses = jnp.zeros((BLK, BLK), F32)
    for r in range(8):
        raw_copies[r].wait()
        degree = jnp.sum(jnp.sum(raw[r].astype(F32), axis=0), axis=1, keepdims=True)
        inverse = lax.rsqrt(degree)
        root[BLK * r : BLK * (r + 1)] = jnp.broadcast_to(inverse, (BLK, WIDE))
        inverses = jnp.where(lane == r, inverse, inverses)
    code_out[16:] = inverses.T[:8]

    pl.semaphore_wait(barrier, len(partners))
    to_left = send(code_out, code_right, halo_send.at[0], halo_recv.at[0], left)
    to_right = send(code_out, code_left, halo_send.at[1], halo_recv.at[1], right)
    relay(0)

    def fill(r):
        half = r % 2
        row = pl.ds(BLK * half, BLK)
        apart = None
        for o in range(9):
            slot, present = places[r][o]
            block = raw[r, slot] * present.astype(BF16)
            if o == BAND:
                block = block.astype(F32)
                inverse = root[BLK * r : BLK * (r + 1), :BLK]
                apart = jnp.sum(jnp.where(diagonal, block, 0.0), axis=1, keepdims=True) * inverse * inverse
                self_part[BLK * r : BLK * (r + 1)] = jnp.concatenate([apart, apart], axis=1)
                block = jnp.where(diagonal, 0.0, block).astype(BF16)
            band[r // 2, row, BLK * (o + half) : BLK * (o + half + 1)] = block
        blank = 9 if half == 0 else 0
        band[r // 2, row, BLK * blank : BLK * (blank + 1)] = jnp.zeros((BLK, BLK), BF16)
        return apart

    def part(i, fields, pairs):
        first, last = pairs
        block = band[i, :, WIDE * (first - i) : WIDE * (last + 1 - i)]
        return sum(
            jnp.dot(block, field[WIDE * first : WIDE * (last + 1)], preferred_element_type=F32) for field in fields
        )

    def split(fields, rows, x):
        high = x.astype(BF16)
        fields[0][rows] = high
        fields[1][rows] = (x - high.astype(F32)).astype(BF16)

    field2, field3 = (field2a, field2b), (field3a, field3b)

    def pair(ref, i):
        return ref.at[pl.ds(WIDE * i, WIDE)]

    def own(fields, i):
        return pair(root, i)[...] * part(i, fields, OWN[i])

    def outward(fields, k, pairs=range(4)):
        return sum(
            jnp.dot(across[t], field[WIDE * (i + 2) : WIDE * (i + 3)], preferred_element_type=F32)
            for t, (i, at) in enumerate(TILES)
            if at == k and i in pairs
            for field in fields
        )

    for r in range(8):
        rows = pl.ds(BLK * r, BLK)
        field1[512 + BLK * r : 512 + BLK * (r + 1)] = (root[rows] * v0[rows]).astype(BF16)
    first = {}
    aparts = jnp.zeros((BLK, BLK), F32)
    for i in (0, 3, 1, 2):
        for r in (2 * i, 2 * i + 1):
            aparts = jnp.where(lane == r, fill(r), aparts)
        partial = own((field1,), i)
        first_out[i] = partial.astype(BF16)
        target, device = (first_in.at[2 + i], left) if i < 2 else (first_in.at[i - 2], right)
        first[i] = send(first_out.at[i], target, halo_send.at[2 + i], halo_recv.at[2 + i], device)
        pair(v1, i)[...] = partial + pair(self_part, i)[...] * pair(v0, i)[...]
    apart_out[...] = aparts.T[:8]
    aparts_left = send(apart_out, apart_right, halo_send.at[8], halo_recv.at[8], left)
    aparts_right = send(apart_out, apart_left, halo_send.at[9], halo_recv.at[9], right)
    relay(1)
    for t, (i, k) in enumerate(TILES):
        across[t] = band[i, :, WIDE * (k - i) : WIDE * (k - i + 1)].T
    for h, k in enumerate(OUTER):
        reach[h] = outward((field1,), k)

    to_left.wait_recv()
    to_right.wait_recv()
    outer = jnp.concatenate([code_left[...], code_right[...], jnp.zeros((BLK - 48, BLK), F32)], axis=0).T
    for e in range(4):
        for at, h, base in ((e, e // 2, 4 + e), (12 + e, 2 + e // 2, 24 + e)):
            rows = pl.ds(BLK * (e % 2), BLK)
            here = jnp.where(column(outer, base + 8, WIDE) == wide_lane, column(outer, base, WIDE), 0.0)
            inverse = column(outer, base + 16, WIDE)
            field1[BLK * at : BLK * (at + 1)] = (inverse * here).astype(BF16)
            outer_root[h, rows] = inverse
            outer_v0[h, rows] = here
    for i in range(4):
        inverse = pair(root, i)[...]
        after = pair(v1, i)[...] + inverse * part(i, (field1,), HALO[i])
        pair(v1, i)[...] = after
        split(field2, pl.ds(512 + WIDE * i, WIDE), inverse * after)

    second = []
    for n, i in enumerate((0, 3)):
        partial = own(field2, i)
        second_out[n] = partial.astype(BF16)
        second.append(
            send(second_out.at[n], second_in.at[1 - n], halo_send.at[6 + n], halo_recv.at[6 + n], (left, right)[n])
        )
        pair(v2, i)[...] = partial + pair(self_part, i)[...] * pair(v1, i)[...]
    relay(2)
    for i in (1, 2):
        pair(v2, i)[...] = own(field2, i) + pair(self_part, i)[...] * pair(v1, i)[...]
    aparts_left.wait_recv()
    aparts_right.wait_recv()
    outer = jnp.concatenate([apart_left[...], apart_right[...], jnp.zeros((BLK - 16, BLK), F32)], axis=0).T
    for e in range(4):
        for h, at in ((e // 2, 4 + e), (2 + e // 2, 8 + e)):
            rows = pl.ds(BLK * (e % 2), BLK)
            apart = column(outer, at, WIDE)
            outer_self[h, rows] = apart
            reach[h, rows] = outer_root[h, rows] * reach[h, rows] + apart * outer_v0[h, rows]
    early = [node_sum(v0[...] * v0[...]), node_sum(v0[...] * v1[...]), node_sum(v1[...] * v1[...])]
    early = scatter(packed(early), part_a, got_a, peers_a, sum_send.at[0], sum_recv.at[0])
    for r in range(8):
        turned1[:, BLK * r : BLK * (r + 1)] = v1[BLK * r : BLK * (r + 1)].T

    for i in (3, 2, 0, 1):
        first[i].wait_recv()
    for h, k in enumerate(OUTER):
        after = first_in[h].astype(F32) + reach[h]
        reach[h] = after
        split(field2, pl.ds(WIDE * k, WIDE), outer_root[h] * after)
    for i in range(4):
        inverse = pair(root, i)[...]
        after = pair(v2, i)[...] + inverse * part(i, field2, HALO[i])
        pair(v2, i)[...] = after
        split(field3, pl.ds(512 + WIDE * i, WIDE), inverse * after)
    sums = [node_sum(v0[...] * v2[...]), node_sum(v1[...] * v2[...]), node_sum(v2[...] * v2[...])]

    relay(3)
    early = scatter(gather(*early), part_b, got_b, peers_b, sum_send.at[1], sum_recv.at[1])

    form = jnp.zeros((1, WIDE), F32)
    for i in range(4):
        field = pair(v2, i)[...]
        form = form + node_sum(field * (own(field3, i) + pair(self_part, i)[...] * field))
    for n, (h, k, pairs) in enumerate(((1, 1, (1,)), (2, 6, (2, 3)))):
        inverse = outer_root[h]
        weight = 2.0 * inverse * outward(field3, k, pairs)
        form = form + node_sum(weight * (inverse * outward(field2, k) + outer_self[h] * reach[h]))
        reach[3 * n] = weight
    for r in range(8):
        turned2[:, BLK * r : BLK * (r + 1)] = v2[BLK * r : BLK * (r + 1)].T
    for n in range(2):
        second[1 - n].wait_recv()
        form = form + node_sum(second_in[n].astype(F32) * reach[3 * n])
    sums.append(form)

    for step in range(4, n_relays + 1):
        relay(step)
    late = scatter(packed(sums), part_all, got_all, peers_all, sum_send.at[2], sum_recv.at[2])
    early = gather(*early)
    late = gather(*late)
    grams = [early[2 * i : 2 * i + 2] for i in range(3)] + [late[2 * i : 2 * i + 2] for i in range(4)]
    weights = combination(grams[:3], grams[3:6], grams[6])
    weights = jnp.concatenate(list(weights) + [jnp.zeros((BLK - 6, BLK), F32)], axis=0).T
    n_classes = seed.shape[0]
    columns = [
        jnp.concatenate([weights[:, 2 * i : 2 * i + 1], weights[:, 2 * i + 1 : 2 * i + 2]], axis=0)[:n_classes]
        for i in range(3)
    ]
    n_lanes = seed.shape[1]
    strength = jnp.zeros((8, n_lanes), F32)
    for at in range(0, n_classes, 8):
        here = slice(at, min(at + 8, n_classes))
        c0, c1, c2 = (jnp.broadcast_to(c[here], (here.stop - at, n_lanes)) for c in columns)
        x = c0 * seed[here] + c1 * turned1[here] + c2 * turned2[here]
        result[here] = x
        if here.stop - at == 8:
            strength = strength + x * x
        else:
            rest = node_sum(x * x)
    strength = node_sum(strength)
    if n_classes % 8:
        strength = strength + rest
    strength = jnp.concatenate([strength[:, BLK * r : BLK * (r + 1)] for r in range(8)], axis=0)
    strength = gather(*scatter(strength, strength_out, strength_in, peers_c, cls_send, cls_recv))
    norm = lax.rsqrt(strength + epsilon)
    for r in range(8):
        here = pl.ds(BLK * r, BLK)
        result[:, here] = result[:, here] * norm[r : r + 1]
    for copy in sent:
        copy.wait_send()
    for got, send_sem in scattered:
        pltpu.make_async_copy(got, got, send_sem).wait()


def shards(n_rows, n_cls, seed_scores, block_columns, affinity):
    n_classes, n_nodes = seed_scores.shape
    n_high = n_rows // GROUP
    field = pltpu.VMEM((2048, WIDE), BF16)
    whole = pltpu.VMEM((1024, WIDE), F32)
    turned = pltpu.VMEM((WIDE, 1024), F32)
    code = pltpu.VMEM((24, BLK), F32)
    tile = pltpu.VMEM((8, BLK), F32)
    outside = pltpu.VMEM((4, WIDE, WIDE), F32)
    return pl.pallas_call(
        functools.partial(kernel, n_rows, n_cls),
        out_shape=jax.ShapeDtypeStruct(seed_scores.shape, F32),
        in_specs=[pl.BlockSpec(memory_space=pl.ANY)] * 3,
        out_specs=pl.BlockSpec(memory_space=pltpu.VMEM),
        scratch_shapes=[
            pltpu.SMEM((8, NNZB), jnp.int32),
            pltpu.VMEM((n_classes, n_nodes), F32),
            pltpu.VMEM((8, NNZB, BLK, BLK), BF16),
            pltpu.VMEM((4, WIDE, 10 * BLK), BF16),
            pltpu.VMEM((len(TILES), WIDE, WIDE), BF16),
            field, field, field, field, field,
            whole, whole, whole, whole, whole,
            outside, outside, outside, outside,
            turned, turned,
            code, code, code, tile, tile, tile,
            pltpu.VMEM((4, WIDE, WIDE), BF16), pltpu.VMEM((4, WIDE, WIDE), BF16),
            pltpu.VMEM((2, WIDE, WIDE), BF16), pltpu.VMEM((2, WIDE, WIDE), BF16),
            tile, tile, tile,
            pltpu.VMEM((GROUP - 1, 8, BLK), F32),
            pltpu.VMEM((max(n_high - 1, 1), 8, BLK), F32),
            pltpu.VMEM((n_rows - 1, 8, BLK), F32),
            tile,
            pltpu.VMEM((max(n_cls - 1, 1), 8, BLK), F32),
            pltpu.SemaphoreType.DMA((10,)),
            pltpu.SemaphoreType.DMA((10,)),
            pltpu.SemaphoreType.DMA((10,)),
            pltpu.SemaphoreType.DMA((3,)),
            pltpu.SemaphoreType.DMA((3,)),
            pltpu.SemaphoreType.DMA,
            pltpu.SemaphoreType.DMA,
            pltpu.SemaphoreType.REGULAR((max(n_high // 2, 1),)),
        ],
        compiler_params=pltpu.CompilerParams(
            collective_id=0, has_side_effects=True, vmem_limit_bytes=VMEM_BYTES
        ),
        cost_estimate=pl.CostEstimate(flops=1600000000, bytes_accessed=4000000, transcendentals=0),
    )(seed_scores, block_columns, affinity)


def solution(mesh):
    return jax.shard_map(
        functools.partial(shards, mesh.shape["rows"], mesh.shape["cls"]),
        mesh=mesh,
        in_specs=(P("cls", "rows"), P("rows", None), P("rows", None, None, None)),
        out_specs=P("cls", "rows"),
        check_vma=False,
    )
```

```python
import functools

import jax
import jax.numpy as jnp
from jax import lax
from jax.experimental import pallas as pl
from jax.experimental.pallas import tpu as pltpu
from jax.sharding import PartitionSpec as P

MESH = pl.DeviceIdType.MESH
BAND = 4
NNZB = 8
BLK = 128
WIDE = 256
GROUP = 8
VMEM_BYTES = 527 * 1024 * 1024 // 10
damping = 0.99
epsilon = 1e-06
F32 = jnp.float32
BF16 = jnp.bfloat16


def column(table, index, width):
    return jnp.broadcast_to(table[:, index : index + 1], (BLK, width))


def node_sum(x):
    return jnp.sum(x, axis=0, keepdims=True)


def ratio(top, bottom):
    good = (bottom > 0) & (top > 0)
    return jnp.where(good, top / jnp.where(good, bottom, 1.0), 0.0)


def combination(early, middle, q):
    g00, g01, g11 = early
    g02, g12, g22 = middle
    g = damping
    gram = [[g00, g01, g02, g12], [g01, g11, g12, g22], [g02, g12, g22, q]]

    def square(p):
        return sum(p[i] * p[j] * gram[i][j] for i in range(len(p)) for j in range(len(p)))

    def energy(p):
        return sum(
            p[i] * p[j] * (gram[i][j] - g * gram[i][j + 1])
            for i in range(len(p))
            for j in range(len(p))
        )

    a0 = ratio(g00, g00 - g * g01)
    r1 = [1.0 - a0, g * a0]
    rr1 = square(r1)
    b0 = ratio(rr1, g00)
    d1 = [r1[0] + b0, r1[1]]
    a1 = ratio(rr1, energy(d1))
    r2 = [r1[0] - a1 * d1[0], r1[1] - a1 * (d1[1] - g * d1[0]), a1 * g * d1[1]]
    rr2 = square(r2)
    b1 = ratio(rr2, rr1)
    d2 = [r2[0] + b1 * d1[0], r2[1] + b1 * d1[1], r2[2]]
    a2 = ratio(rr2, energy(d2))
    return a0 + a1 * d1[0] + a2 * d2[0], a1 * d1[1] + a2 * d2[1], a2 * d2[2]


OWN = {i: (max(i, 2), min(i + 4, 5)) for i in range(4)}
HALO = {0: (0, 1), 1: (1, 1), 2: (6, 6), 3: (6, 7)}
OUTER = (0, 1, 6, 7)
TILES = ((0, 0), (0, 1), (1, 1), (2, 6), (3, 6), (3, 7))


def kernel(
    n_rows, n_cls,
    seed_hbm, columns_hbm, affinity_hbm, result,
    columns_ref, seed, raw, band, across, field1, field2a, field2b, field3a, field3b, v0, v1, v2, root, self_part, outer_root, outer_v0, outer_self,
    reach, turned1, turned2,
    code_out, code_left, code_right, apart_out, apart_left, apart_right, first_out, first_in, second_out, second_in,
    part_a, part_b, got_a, got_b, strength_out, strength_in,
    load_sem, halo_send, halo_recv, sum_send, sum_recv, cls_send, cls_recv, relay_sem,
):
    me = lax.axis_index("rows")
    mine = lax.axis_index("cls")
    low, high = lax.rem(me, GROUP), me // GROUP
    n_high = n_rows // GROUP
    total_blocks = n_rows * 8

    columns_copy = pltpu.make_async_copy(columns_hbm, columns_ref, load_sem.at[9])
    columns_copy.start()
    seed_copy = pltpu.make_async_copy(seed_hbm, seed, load_sem.at[8])
    seed_copy.start()
    raw_copies = []
    for r in range(8):
        copy = pltpu.make_async_copy(affinity_hbm.at[r], raw.at[r], load_sem.at[r])
        copy.start()
        raw_copies.append(copy)

    left = {"rows": lax.rem(me + n_rows - 1, n_rows), "cls": mine}
    right = {"rows": lax.rem(me + 1, n_rows), "cls": mine}
    far = sorted(range(1, GROUP), key=lambda d: -min(d, GROUP - d))
    peers_a = [{"rows": high * GROUP + lax.rem(low + d, GROUP), "cls": mine} for d in far]
    peers_b = [{"rows": lax.rem(high + d, n_high) * GROUP + low, "cls": mine} for d in range(1, n_high)]
    far = sorted(range(1, n_cls), key=lambda d: -min(d, n_cls - d))
    peers_c = [{"rows": me, "cls": lax.rem(mine + d, n_cls)} for d in far]
    barrier = pltpu.get_barrier_semaphore()
    above = {"rows": lax.rem(high + 1, n_high) * GROUP + low, "cls": mine}
    below = {"rows": lax.rem(high + n_high - 1, n_high) * GROUP + low, "cls": mine}
    partners = [left, right] + [above, below] + peers_a + peers_c
    for device in partners:
        pl.semaphore_signal(barrier, inc=1, device_id=device, device_id_type=MESH)

    sent = []

    def send(source, target, send_sem, recv_sem, device):
        copy = pltpu.make_async_remote_copy(
            src_ref=source, dst_ref=target, send_sem=send_sem, recv_sem=recv_sem,
            device_id=device, device_id_type=MESH,
        )
        copy.start()
        sent.append(copy)
        return copy

    def packed(sums):
        pieces = [half for x in sums for half in (x[:, :BLK], x[:, BLK:])]
        pieces.append(jnp.zeros((16 - len(pieces), BLK), F32))
        return jnp.concatenate(pieces, axis=0)

    def scatter(tile, out, got, peers, send_sem, recv_sem):
        out[...] = tile
        for d, device in enumerate(peers):
            copy = pltpu.make_async_remote_copy(
                src_ref=out, dst_ref=got.at[d], send_sem=send_sem, recv_sem=recv_sem,
                device_id=device, device_id_type=MESH,
            )
            copy.start()
        if peers:
            scattered.append((got, send_sem))
        return tile, got, peers, recv_sem

    def gather(tile, got, peers, recv_sem):
        if peers:
            pltpu.make_async_copy(got, got, recv_sem).wait()
            tile = tile + jnp.sum(got[...], axis=0)
        return tile

    scattered = []

    n_relays = max(n_high // 2 - 1, 0)

    def relay(step):
        if 0 < step <= n_relays:
            pl.semaphore_wait(relay_sem.at[step - 1], 2)
        if step < n_relays:
            for device in (above, below):
                pl.semaphore_signal(relay_sem.at[step], inc=1, device_id=device, device_id_type=MESH)

    lane = lax.broadcasted_iota(jnp.int32, (BLK, BLK), 1)
    diagonal = lane == lax.broadcasted_iota(jnp.int32, (BLK, BLK), 0)
    wide_lane = lax.broadcasted_iota(jnp.int32, (BLK, WIDE), 1).astype(F32)
    columns_copy.wait()
    places = []
    for r in range(8):
        offsets = [
            lax.rem(columns_ref[r, j] - (me * 8 + r) + BAND + total_blocks, total_blocks) for j in range(NNZB)
        ]
        absent = sum(range(9)) - sum(offsets)
        slots = []
        for o in range(9):
            j = 0
            for i in range(1, NNZB):
                j = jnp.where(offsets[i] == o, i, j)
            slots.append((j, (absent != o).astype(F32)))
        places.append(slots)

    seed_copy.wait()
    scores = seed[...]
    class_id = lax.broadcasted_iota(jnp.int32, scores.shape, 0).astype(F32)
    value = node_sum(scores)
    label = node_sum(jnp.where(scores > 0, class_id, 0.0))
    rows = [value[:, BLK * r : BLK * (r + 1)] for r in range(8)]
    rows += [label[:, BLK * r : BLK * (r + 1)] for r in range(8)]
    rows = jnp.concatenate(rows, axis=0)
    code_out[:16] = rows
    code = jnp.concatenate([rows, jnp.zeros((BLK - 16, BLK), F32)], axis=0).T
    for r in range(8):
        v0[BLK * r : BLK * (r + 1)] = jnp.where(
            column(code, 8 + r, WIDE) == wide_lane, column(code, r, WIDE), 0.0
        )

    inverses = jnp.zeros((BLK, BLK), F32)
    for r in range(8):
        raw_copies[r].wait()
        degree = jnp.sum(jnp.sum(raw[r].astype(F32), axis=0), axis=1, keepdims=True)
        inverse = lax.rsqrt(degree)
        root[BLK * r : BLK * (r + 1)] = jnp.broadcast_to(inverse, (BLK, WIDE))
        inverses = jnp.where(lane == r, inverse, inverses)
    code_out[16:] = inverses.T[:8]

    pl.semaphore_wait(barrier, len(partners))
    to_left = send(code_out, code_right, halo_send.at[0], halo_recv.at[0], left)
    to_right = send(code_out, code_left, halo_send.at[1], halo_recv.at[1], right)
    relay(0)

    def fill(r):
        half = r % 2
        row = pl.ds(BLK * half, BLK)
        apart = None
        for o in range(9):
            slot, present = places[r][o]
            block = raw[r, slot] * present.astype(BF16)
            if o == BAND:
                block = block.astype(F32)
                inverse = root[BLK * r : BLK * (r + 1), :BLK]
                apart = jnp.sum(jnp.where(diagonal, block, 0.0), axis=1, keepdims=True) * inverse * inverse
                self_part[BLK * r : BLK * (r + 1)] = jnp.concatenate([apart, apart], axis=1)
                block = jnp.where(diagonal, 0.0, block).astype(BF16)
            band[r // 2, row, BLK * (o + half) : BLK * (o + half + 1)] = block
        blank = 9 if half == 0 else 0
        band[r // 2, row, BLK * blank : BLK * (blank + 1)] = jnp.zeros((BLK, BLK), BF16)
        return apart

    def part(i, fields, pairs):
        first, last = pairs
        block = band[i, :, WIDE * (first - i) : WIDE * (last + 1 - i)]
        return sum(
            jnp.dot(block, field[WIDE * first : WIDE * (last + 1)], preferred_element_type=F32) for field in fields
        )

    def split(fields, rows, x):
        high = x.astype(BF16)
        fields[0][rows] = high
        fields[1][rows] = (x - high.astype(F32)).astype(BF16)

    field2, field3 = (field2a, field2b), (field3a, field3b)

    def pair(ref, i):
        return ref.at[pl.ds(WIDE * i, WIDE)]

    def own(fields, i):
        return pair(root, i)[...] * part(i, fields, OWN[i])

    def outward(fields, k, pairs=range(4)):
        return sum(
            jnp.dot(across[t], field[WIDE * (i + 2) : WIDE * (i + 3)], preferred_element_type=F32)
            for t, (i, at) in enumerate(TILES)
            if at == k and i in pairs
            for field in fields
        )

    for r in range(8):
        rows = pl.ds(BLK * r, BLK)
        field1[512 + BLK * r : 512 + BLK * (r + 1)] = (root[rows] * v0[rows]).astype(BF16)
    first = {}
    aparts = jnp.zeros((BLK, BLK), F32)
    for i in (0, 3, 1, 2):
        for r in (2 * i, 2 * i + 1):
            aparts = jnp.where(lane == r, fill(r), aparts)
        partial = own((field1,), i)
        first_out[i] = partial.astype(BF16)
        target, device = (first_in.at[2 + i], left) if i < 2 else (first_in.at[i - 2], right)
        first[i] = send(first_out.at[i], target, halo_send.at[2 + i], halo_recv.at[2 + i], device)
        pair(v1, i)[...] = partial + pair(self_part, i)[...] * pair(v0, i)[...]
    apart_out[...] = aparts.T[:8]
    aparts_left = send(apart_out, apart_right, halo_send.at[8], halo_recv.at[8], left)
    aparts_right = send(apart_out, apart_left, halo_send.at[9], halo_recv.at[9], right)
    relay(1)
    for t, (i, k) in enumerate(TILES):
        across[t] = band[i, :, WIDE * (k - i) : WIDE * (k - i + 1)].T
    for h, k in enumerate(OUTER):
        reach[h] = outward((field1,), k)

    to_left.wait_recv()
    to_right.wait_recv()
    outer = jnp.concatenate([code_left[...], code_right[...], jnp.zeros((BLK - 48, BLK), F32)], axis=0).T
    for e in range(4):
        for at, h, base in ((e, e // 2, 4 + e), (12 + e, 2 + e // 2, 24 + e)):
            rows = pl.ds(BLK * (e % 2), BLK)
            here = jnp.where(column(outer, base + 8, WIDE) == wide_lane, column(outer, base, WIDE), 0.0)
            inverse = column(outer, base + 16, WIDE)
            field1[BLK * at : BLK * (at + 1)] = (inverse * here).astype(BF16)
            outer_root[h, rows] = inverse
            outer_v0[h, rows] = here
    for i in range(4):
        inverse = pair(root, i)[...]
        after = pair(v1, i)[...] + inverse * part(i, (field1,), HALO[i])
        pair(v1, i)[...] = after
        field2a[512 + WIDE * i : 512 + WIDE * (i + 1)] = (inverse * after).astype(BF16)

    second = []
    for n, i in enumerate((0, 3)):
        partial = own((field2a,), i)
        second_out[n] = partial.astype(BF16)
        second.append(
            send(second_out.at[n], second_in.at[1 - n], halo_send.at[6 + n], halo_recv.at[6 + n], (left, right)[n])
        )
        pair(v2, i)[...] = partial
    relay(2)
    for i in range(4):
        rows = pl.ds(512 + WIDE * i, WIDE)
        low_part = pair(root, i)[...] * pair(v1, i)[...] - field2a[rows].astype(F32)
        field2b[rows] = low_part.astype(BF16)
    for i in range(4):
        partial = own((field2b,), i) + pair(v2, i)[...] if i in (0, 3) else own(field2, i)
        pair(v2, i)[...] = partial + pair(self_part, i)[...] * pair(v1, i)[...]
    aparts_left.wait_recv()
    aparts_right.wait_recv()
    outer = jnp.concatenate([apart_left[...], apart_right[...], jnp.zeros((BLK - 16, BLK), F32)], axis=0).T
    for e in range(4):
        for h, at in ((e // 2, 4 + e), (2 + e // 2, 8 + e)):
            rows = pl.ds(BLK * (e % 2), BLK)
            apart = column(outer, at, WIDE)
            outer_self[h, rows] = apart
            reach[h, rows] = outer_root[h, rows] * reach[h, rows] + apart * outer_v0[h, rows]
    sums = [node_sum(v0[...] * v0[...]), node_sum(v0[...] * v1[...]), node_sum(v1[...] * v1[...])]
    for i in (3, 2, 0, 1):
        first[i].wait_recv()
    for h, k in enumerate(OUTER):
        after = first_in[h].astype(F32) + reach[h]
        reach[h] = after
        split(field2, pl.ds(WIDE * k, WIDE), outer_root[h] * after)
    late = [jnp.zeros((1, WIDE), F32)] * 3
    for i in range(4):
        inverse = pair(root, i)[...]
        after = pair(v2, i)[...] + inverse * part(i, field2, HALO[i])
        pair(v2, i)[...] = after
        split(field3, pl.ds(512 + WIDE * i, WIDE), inverse * after)
        late[0] = late[0] + node_sum(pair(v0, i)[...] * after)
        late[1] = late[1] + node_sum(pair(v1, i)[...] * after)
        late[2] = late[2] + node_sum(after * after)
    sums += late

    form = jnp.zeros((1, WIDE), F32)
    for i in range(4):
        field = pair(v2, i)[...]
        form = form + node_sum(field * (own(field3, i) + pair(self_part, i)[...] * field))
    for n, (h, k, pairs) in enumerate(((1, 1, (1,)), (2, 6, (2, 3)))):
        inverse = outer_root[h]
        weight = 2.0 * inverse * outward(field3, k, pairs)
        form = form + node_sum(weight * (inverse * outward(field2, k) + outer_self[h] * reach[h]))
        reach[3 * n] = weight
    for n in range(2):
        second[1 - n].wait_recv()
        form = form + node_sum(second_in[n].astype(F32) * reach[3 * n])
    sums.append(form)

    tile = scatter(packed(sums), part_a, got_a, peers_a, sum_send.at[0], sum_recv.at[0])
    for r in range(8):
        turned1[:, BLK * r : BLK * (r + 1)] = v1[BLK * r : BLK * (r + 1)].T
    tile = gather(*tile)
    relay(3)
    tile = scatter(tile, part_b, got_b, peers_b, sum_send.at[1], sum_recv.at[1])
    for r in range(8):
        turned2[:, BLK * r : BLK * (r + 1)] = v2[BLK * r : BLK * (r + 1)].T
    tile = gather(*tile)
    grams = [tile[2 * i : 2 * i + 2] for i in range(7)]
    weights = combination(grams[:3], grams[3:6], grams[6])
    weights = jnp.concatenate(list(weights) + [jnp.zeros((BLK - 6, BLK), F32)], axis=0).T
    n_classes = seed.shape[0]
    columns = [
        jnp.concatenate([weights[:, 2 * i : 2 * i + 1], weights[:, 2 * i + 1 : 2 * i + 2]], axis=0)[:n_classes]
        for i in range(3)
    ]
    n_lanes = seed.shape[1]
    strength = jnp.zeros((8, n_lanes), F32)
    for at in range(0, n_classes, 8):
        here = slice(at, min(at + 8, n_classes))
        c0, c1, c2 = (jnp.broadcast_to(c[here], (here.stop - at, n_lanes)) for c in columns)
        x = c0 * seed[here] + c1 * turned1[here] + c2 * turned2[here]
        result[here] = x
        if here.stop - at == 8:
            strength = strength + x * x
        else:
            rest = node_sum(x * x)
    strength = node_sum(strength)
    if n_classes % 8:
        strength = strength + rest
    strength = jnp.concatenate([strength[:, BLK * r : BLK * (r + 1)] for r in range(8)], axis=0)
    strength = gather(*scatter(strength, strength_out, strength_in, peers_c, cls_send, cls_recv))
    norm = lax.rsqrt(strength + epsilon)
    for r in range(8):
        here = pl.ds(BLK * r, BLK)
        result[:, here] = result[:, here] * norm[r : r + 1]
    for copy in sent:
        copy.wait_send()
    for got, send_sem in scattered:
        pltpu.make_async_copy(got, got, send_sem).wait()


def shards(n_rows, n_cls, seed_scores, block_columns, affinity):
    n_classes, n_nodes = seed_scores.shape
    n_high = n_rows // GROUP
    field = pltpu.VMEM((2048, WIDE), BF16)
    whole = pltpu.VMEM((1024, WIDE), F32)
    turned = pltpu.VMEM((WIDE, 1024), F32)
    code = pltpu.VMEM((24, BLK), F32)
    tile = pltpu.VMEM((8, BLK), F32)
    sums = pltpu.VMEM((16, BLK), F32)
    outside = pltpu.VMEM((4, WIDE, WIDE), F32)
    return pl.pallas_call(
        functools.partial(kernel, n_rows, n_cls),
        out_shape=jax.ShapeDtypeStruct(seed_scores.shape, F32),
        in_specs=[pl.BlockSpec(memory_space=pl.ANY)] * 3,
        out_specs=pl.BlockSpec(memory_space=pltpu.VMEM),
        scratch_shapes=[
            pltpu.SMEM((8, NNZB), jnp.int32),
            pltpu.VMEM((n_classes, n_nodes), F32),
            pltpu.VMEM((8, NNZB, BLK, BLK), BF16),
            pltpu.VMEM((4, WIDE, 10 * BLK), BF16),
            pltpu.VMEM((len(TILES), WIDE, WIDE), BF16),
            field, field, field, field, field,
            whole, whole, whole, whole, whole,
            outside, outside, outside, outside,
            turned, turned,
            code, code, code, tile, tile, tile,
            pltpu.VMEM((4, WIDE, WIDE), BF16), pltpu.VMEM((4, WIDE, WIDE), BF16),
            pltpu.VMEM((2, WIDE, WIDE), BF16), pltpu.VMEM((2, WIDE, WIDE), BF16),
            sums, sums,
            pltpu.VMEM((GROUP - 1, 16, BLK), F32),
            pltpu.VMEM((max(n_high - 1, 1), 16, BLK), F32),
            tile,
            pltpu.VMEM((max(n_cls - 1, 1), 8, BLK), F32),
            pltpu.SemaphoreType.DMA((10,)),
            pltpu.SemaphoreType.DMA((10,)),
            pltpu.SemaphoreType.DMA((10,)),
            pltpu.SemaphoreType.DMA((2,)),
            pltpu.SemaphoreType.DMA((2,)),
            pltpu.SemaphoreType.DMA,
            pltpu.SemaphoreType.DMA,
            pltpu.SemaphoreType.REGULAR((max(n_high // 2 - 1, 1),)),
        ],
        compiler_params=pltpu.CompilerParams(
            collective_id=0, has_side_effects=True, vmem_limit_bytes=VMEM_BYTES
        ),
        cost_estimate=pl.CostEstimate(flops=1600000000, bytes_accessed=4000000, transcendentals=0),
    )(seed_scores, block_columns, affinity)


def solution(mesh):
    return jax.shard_map(
        functools.partial(shards, mesh.shape["rows"], mesh.shape["cls"]),
        mesh=mesh,
        in_specs=(P("cls", "rows"), P("rows", None), P("rows", None, None, None)),
        out_specs=P("cls", "rows"),
        check_vma=False,
    )
```

```python
import functools

import jax
import jax.numpy as jnp
from jax import lax
from jax.experimental import pallas as pl
from jax.experimental.pallas import tpu as pltpu
from jax.sharding import PartitionSpec as P

MESH = pl.DeviceIdType.MESH
BAND = 4
NNZB = 8
BLK = 128
WIDE = 256
GROUP = 8
VMEM_BYTES = 527 * 1024 * 1024 // 10
damping = 0.99
epsilon = 1e-06
F32 = jnp.float32
BF16 = jnp.bfloat16


def column(table, index, width):
    return jnp.broadcast_to(table[:, index : index + 1], (BLK, width))


def node_sum(x):
    return jnp.sum(x, axis=0, keepdims=True)


def ratio(top, bottom):
    good = (bottom > 0) & (top > 0)
    return jnp.where(good, top / jnp.where(good, bottom, 1.0), 0.0)


def combination(early, middle, q):
    g00, g01, g11 = early
    g02, g12, g22 = middle
    g = damping
    gram = [[g00, g01, g02, g12], [g01, g11, g12, g22], [g02, g12, g22, q]]

    def square(p):
        return sum(p[i] * p[j] * gram[i][j] for i in range(len(p)) for j in range(len(p)))

    def energy(p):
        return sum(
            p[i] * p[j] * (gram[i][j] - g * gram[i][j + 1])
            for i in range(len(p))
            for j in range(len(p))
        )

    a0 = ratio(g00, g00 - g * g01)
    r1 = [1.0 - a0, g * a0]
    rr1 = square(r1)
    b0 = ratio(rr1, g00)
    d1 = [r1[0] + b0, r1[1]]
    a1 = ratio(rr1, energy(d1))
    r2 = [r1[0] - a1 * d1[0], r1[1] - a1 * (d1[1] - g * d1[0]), a1 * g * d1[1]]
    rr2 = square(r2)
    b1 = ratio(rr2, rr1)
    d2 = [r2[0] + b1 * d1[0], r2[1] + b1 * d1[1], r2[2]]
    a2 = ratio(rr2, energy(d2))
    return a0 + a1 * d1[0] + a2 * d2[0], a1 * d1[1] + a2 * d2[1], a2 * d2[2]


OWN = {i: (max(i, 2), min(i + 4, 5)) for i in range(4)}
HALO = {0: (0, 1), 1: (1, 1), 2: (6, 6), 3: (6, 7)}
OUTER = (0, 1, 6, 7)
TILES = ((0, 0), (0, 1), (1, 1), (2, 6), (3, 6), (3, 7))


def kernel(
    n_rows, n_cls,
    seed_hbm, columns_hbm, affinity_hbm, result,
    columns_ref, seed, raw, band, across, field1, field2a, field2b, field3a, field3b, v0, v1, v2, root, self_part, outer_root, outer_v0, outer_self,
    reach, turned1, turned2,
    code_out, code_left, code_right, apart_out, apart_left, apart_right, first_out, first_in, second_out, second_in,
    part_a, part_b, got_a, got_b, strength_out, strength_in,
    load_sem, halo_send, halo_recv, sum_send, sum_recv, cls_send, cls_recv, relay_sem,
):
    me = lax.axis_index("rows")
    mine = lax.axis_index("cls")
    low, high = lax.rem(me, GROUP), me // GROUP
    n_high = n_rows // GROUP
    total_blocks = n_rows * 8

    columns_copy = pltpu.make_async_copy(columns_hbm, columns_ref, load_sem.at[9])
    columns_copy.start()
    seed_copy = pltpu.make_async_copy(seed_hbm, seed, load_sem.at[8])
    seed_copy.start()
    raw_copies = []
    for r in range(8):
        copy = pltpu.make_async_copy(affinity_hbm.at[r], raw.at[r], load_sem.at[r])
        copy.start()
        raw_copies.append(copy)

    left = {"rows": lax.rem(me + n_rows - 1, n_rows), "cls": mine}
    right = {"rows": lax.rem(me + 1, n_rows), "cls": mine}
    far = sorted(range(1, GROUP), key=lambda d: -min(d, GROUP - d))
    peers_a = [{"rows": high * GROUP + lax.rem(low + d, GROUP), "cls": mine} for d in far]
    peers_b = [{"rows": lax.rem(high + d, n_high) * GROUP + low, "cls": mine} for d in range(1, n_high)]
    far = sorted(range(1, n_cls), key=lambda d: -min(d, n_cls - d))
    peers_c = [{"rows": me, "cls": lax.rem(mine + d, n_cls)} for d in far]
    barrier = pltpu.get_barrier_semaphore()
    above = {"rows": lax.rem(high + 1, n_high) * GROUP + low, "cls": mine}
    below = {"rows": lax.rem(high + n_high - 1, n_high) * GROUP + low, "cls": mine}
    core = lax.rem(low, 2)
    beside = [
        {"rows": high * GROUP + lax.rem(low + step, GROUP), "cls": mine} for step in (2, GROUP - 2)
    ] + [{"rows": me, "cls": lax.rem(mine + step, n_cls)} for step in (1, n_cls - 1)] + [above, below]
    crossed = [
        {"rows": high * GROUP + lax.rem(low + 1 - 2 * core + step, GROUP), "cls": mine} for step in (GROUP, GROUP + 2, GROUP - 2)
    ]
    partners = [left, right] + beside + crossed
    for device in partners:
        pl.semaphore_signal(barrier, inc=1, device_id=device, device_id_type=MESH)

    sent = []

    def send(source, target, send_sem, recv_sem, device):
        copy = pltpu.make_async_remote_copy(
            src_ref=source, dst_ref=target, send_sem=send_sem, recv_sem=recv_sem,
            device_id=device, device_id_type=MESH,
        )
        copy.start()
        sent.append(copy)
        return copy

    def packed(sums):
        pieces = [half for x in sums for half in (x[:, :BLK], x[:, BLK:])]
        pieces.append(jnp.zeros((16 - len(pieces), BLK), F32))
        return jnp.concatenate(pieces, axis=0)

    def scatter(tile, out, got, peers, send_sem, recv_sem):
        out[...] = tile
        for d, device in enumerate(peers):
            copy = pltpu.make_async_remote_copy(
                src_ref=out, dst_ref=got.at[d], send_sem=send_sem, recv_sem=recv_sem,
                device_id=device, device_id_type=MESH,
            )
            copy.start()
        if peers:
            scattered.append((got, send_sem))
        return tile, got, peers, recv_sem

    def gather(tile, got, peers, recv_sem):
        if peers:
            pltpu.make_async_copy(got, got, recv_sem).wait()
            tile = tile + jnp.sum(got[...], axis=0)
        return tile

    scattered = []

    n_relays = max(n_high // 2 - 1, 1)

    def relay(step):
        if 0 < step <= n_relays:
            pl.semaphore_wait(relay_sem.at[step - 1], len(beside) if step == 1 else 2)
        if step < n_relays:
            for device in beside if step == 0 else (above, below):
                pl.semaphore_signal(relay_sem.at[step], inc=1, device_id=device, device_id_type=MESH)

    lane = lax.broadcasted_iota(jnp.int32, (BLK, BLK), 1)
    diagonal = lane == lax.broadcasted_iota(jnp.int32, (BLK, BLK), 0)
    wide_lane = lax.broadcasted_iota(jnp.int32, (BLK, WIDE), 1).astype(F32)
    columns_copy.wait()
    places = []
    for r in range(8):
        offsets = [
            lax.rem(columns_ref[r, j] - (me * 8 + r) + BAND + total_blocks, total_blocks) for j in range(NNZB)
        ]
        absent = sum(range(9)) - sum(offsets)
        slots = []
        for o in range(9):
            j = 0
            for i in range(1, NNZB):
                j = jnp.where(offsets[i] == o, i, j)
            slots.append((j, (absent != o).astype(F32)))
        places.append(slots)

    seed_copy.wait()
    scores = seed[...]
    class_id = lax.broadcasted_iota(jnp.int32, scores.shape, 0).astype(F32)
    value = node_sum(scores)
    label = node_sum(jnp.where(scores > 0, class_id, 0.0))
    rows = [value[:, BLK * r : BLK * (r + 1)] for r in range(8)]
    rows += [label[:, BLK * r : BLK * (r + 1)] for r in range(8)]
    rows = jnp.concatenate(rows, axis=0)
    code_out[:16] = rows
    code = jnp.concatenate([rows, jnp.zeros((BLK - 16, BLK), F32)], axis=0).T
    for r in range(8):
        v0[BLK * r : BLK * (r + 1)] = jnp.where(
            column(code, 8 + r, WIDE) == wide_lane, column(code, r, WIDE), 0.0
        )

    for copy in raw_copies:
        copy.wait()
    inverses = jnp.zeros((BLK, BLK), F32)
    for r in range(8):
        degree = jnp.sum(jnp.sum(raw[r].astype(F32), axis=0), axis=1, keepdims=True)
        inverse = lax.rsqrt(degree)
        root[BLK * r : BLK * (r + 1)] = jnp.broadcast_to(inverse, (BLK, WIDE))
        inverses = jnp.where(lane == r, inverse, inverses)
    code_out[16:] = inverses.T[:8]

    pl.semaphore_wait(barrier, len(partners))
    to_left = send(code_out, code_right, halo_send.at[0], halo_recv.at[0], left)
    to_right = send(code_out, code_left, halo_send.at[1], halo_recv.at[1], right)
    relay(0)

    def fill(r):
        half = r % 2
        row = pl.ds(BLK * half, BLK)
        apart = None
        for o in range(9):
            slot, present = places[r][o]
            block = raw[r, slot] * present.astype(BF16)
            if o == BAND:
                block = block.astype(F32)
                inverse = root[BLK * r : BLK * (r + 1), :BLK]
                apart = jnp.sum(jnp.where(diagonal, block, 0.0), axis=1, keepdims=True) * inverse * inverse
                self_part[BLK * r : BLK * (r + 1)] = jnp.concatenate([apart, apart], axis=1)
                block = jnp.where(diagonal, 0.0, block).astype(BF16)
            band[r // 2, row, BLK * (o + half) : BLK * (o + half + 1)] = block
        blank = 9 if half == 0 else 0
        band[r // 2, row, BLK * blank : BLK * (blank + 1)] = jnp.zeros((BLK, BLK), BF16)
        return apart

    def part(i, fields, pairs):
        first, last = pairs
        block = band[i, :, WIDE * (first - i) : WIDE * (last + 1 - i)]
        return sum(
            jnp.dot(block, field[WIDE * first : WIDE * (last + 1)], preferred_element_type=F32) for field in fields
        )

    def split(fields, rows, x):
        high = x.astype(BF16)
        fields[0][rows] = high
        fields[1][rows] = (x - high.astype(F32)).astype(BF16)

    field2, field3 = (field2a, field2b), (field3a, field3b)

    def pair(ref, i):
        return ref.at[pl.ds(WIDE * i, WIDE)]

    def own(fields, i):
        return pair(root, i)[...] * part(i, fields, OWN[i])

    def outward(fields, k, pairs=range(4)):
        return sum(
            jnp.dot(across[t], field[WIDE * (i + 2) : WIDE * (i + 3)], preferred_element_type=F32)
            for t, (i, at) in enumerate(TILES)
            if at == k and i in pairs
            for field in fields
        )

    for r in range(8):
        rows = pl.ds(BLK * r, BLK)
        field1[512 + BLK * r : 512 + BLK * (r + 1)] = (root[rows] * v0[rows]).astype(BF16)
    first = {}
    aparts = jnp.zeros((BLK, BLK), F32)
    for i in (0, 3, 1, 2):
        for r in (2 * i, 2 * i + 1):
            aparts = jnp.where(lane == r, fill(r), aparts)
        partial = own((field1,), i)
        first_out[i] = partial.astype(BF16)
        target, device = (first_in.at[2 + i], left) if i < 2 else (first_in.at[i - 2], right)
        first[i] = send(first_out.at[i], target, halo_send.at[2 + i], halo_recv.at[2 + i], device)
        pair(v1, i)[...] = partial + pair(self_part, i)[...] * pair(v0, i)[...]
    apart_out[...] = aparts.T[:8]
    aparts_left = send(apart_out, apart_right, halo_send.at[8], halo_recv.at[8], left)
    aparts_right = send(apart_out, apart_left, halo_send.at[9], halo_recv.at[9], right)
    relay(1)
    for t, (i, k) in enumerate(TILES):
        across[t] = band[i, :, WIDE * (k - i) : WIDE * (k - i + 1)].T
    for h, k in enumerate(OUTER):
        reach[h] = outward((field1,), k)

    to_left.wait_recv()
    to_right.wait_recv()
    outer = jnp.concatenate([code_left[...], code_right[...], jnp.zeros((BLK - 48, BLK), F32)], axis=0).T
    for e in range(4):
        for at, h, base in ((e, e // 2, 4 + e), (12 + e, 2 + e // 2, 24 + e)):
            rows = pl.ds(BLK * (e % 2), BLK)
            here = jnp.where(column(outer, base + 8, WIDE) == wide_lane, column(outer, base, WIDE), 0.0)
            inverse = column(outer, base + 16, WIDE)
            field1[BLK * at : BLK * (at + 1)] = (inverse * here).astype(BF16)
            outer_root[h, rows] = inverse
            outer_v0[h, rows] = here
    for i in range(4):
        inverse = pair(root, i)[...]
        after = pair(v1, i)[...] + inverse * part(i, (field1,), HALO[i])
        pair(v1, i)[...] = after
        field2a[512 + WIDE * i : 512 + WIDE * (i + 1)] = (inverse * after).astype(BF16)

    second = []
    for n, i in enumerate((0, 3)):
        partial = own((field2a,), i)
        second_out[n] = partial.astype(BF16)
        second.append(
            send(second_out.at[n], second_in.at[1 - n], halo_send.at[6 + n], halo_recv.at[6 + n], (left, right)[n])
        )
        pair(v2, i)[...] = partial
    relay(2)
    for i in range(4):
        rows = pl.ds(512 + WIDE * i, WIDE)
        low_part = pair(root, i)[...] * pair(v1, i)[...] - field2a[rows].astype(F32)
        field2b[rows] = low_part.astype(BF16)
    for i in range(4):
        partial = own((field2b,), i) + pair(v2, i)[...] if i in (0, 3) else own(field2, i)
        pair(v2, i)[...] = partial + pair(self_part, i)[...] * pair(v1, i)[...]
    aparts_left.wait_recv()
    aparts_right.wait_recv()
    outer = jnp.concatenate([apart_left[...], apart_right[...], jnp.zeros((BLK - 16, BLK), F32)], axis=0).T
    for e in range(4):
        for h, at in ((e // 2, 4 + e), (2 + e // 2, 8 + e)):
            rows = pl.ds(BLK * (e % 2), BLK)
            apart = column(outer, at, WIDE)
            outer_self[h, rows] = apart
            reach[h, rows] = outer_root[h, rows] * reach[h, rows] + apart * outer_v0[h, rows]
    sums = [node_sum(v0[...] * v0[...]), node_sum(v0[...] * v1[...]), node_sum(v1[...] * v1[...])]
    for i in (3, 2, 0, 1):
        first[i].wait_recv()
    for h, k in enumerate(OUTER):
        after = first_in[h].astype(F32) + reach[h]
        reach[h] = after
        split(field2, pl.ds(WIDE * k, WIDE), outer_root[h] * after)
    late = [jnp.zeros((1, WIDE), F32)] * 3
    for i in range(4):
        inverse = pair(root, i)[...]
        after = pair(v2, i)[...] + inverse * part(i, field2, HALO[i])
        pair(v2, i)[...] = after
        split(field3, pl.ds(512 + WIDE * i, WIDE), inverse * after)
        late[0] = late[0] + node_sum(pair(v0, i)[...] * after)
        late[1] = late[1] + node_sum(pair(v1, i)[...] * after)
        late[2] = late[2] + node_sum(after * after)
    sums += late

    form = jnp.zeros((1, WIDE), F32)
    for i in range(4):
        field = pair(v2, i)[...]
        form = form + node_sum(field * (own(field3, i) + pair(self_part, i)[...] * field))
    for n, (h, k, pairs) in enumerate(((1, 1, (1,)), (2, 6, (2, 3)))):
        inverse = outer_root[h]
        weight = 2.0 * inverse * outward(field3, k, pairs)
        form = form + node_sum(weight * (inverse * outward(field2, k) + outer_self[h] * reach[h]))
        reach[3 * n] = weight
    for n in range(2):
        second[1 - n].wait_recv()
        form = form + node_sum(second_in[n].astype(F32) * reach[3 * n])
    sums.append(form)

    tile = scatter(packed(sums), part_a, got_a, peers_a, sum_send.at[0], sum_recv.at[0])
    for r in range(8):
        turned1[:, BLK * r : BLK * (r + 1)] = v1[BLK * r : BLK * (r + 1)].T
    tile = gather(*tile)
    relay(3)
    tile = scatter(tile, part_b, got_b, peers_b, sum_send.at[1], sum_recv.at[1])
    for r in range(8):
        turned2[:, BLK * r : BLK * (r + 1)] = v2[BLK * r : BLK * (r + 1)].T
    tile = gather(*tile)
    grams = [tile[2 * i : 2 * i + 2] for i in range(7)]
    weights = combination(grams[:3], grams[3:6], grams[6])
    weights = jnp.concatenate(list(weights) + [jnp.zeros((BLK - 6, BLK), F32)], axis=0).T
    n_classes = seed.shape[0]
    columns = [
        jnp.concatenate([weights[:, 2 * i : 2 * i + 1], weights[:, 2 * i + 1 : 2 * i + 2]], axis=0)[:n_classes]
        for i in range(3)
    ]
    n_lanes = seed.shape[1]
    strength = jnp.zeros((8, n_lanes), F32)
    for at in range(0, n_classes, 8):
        here = slice(at, min(at + 8, n_classes))
        c0, c1, c2 = (jnp.broadcast_to(c[here], (here.stop - at, n_lanes)) for c in columns)
        x = c0 * seed[here] + c1 * turned1[here] + c2 * turned2[here]
        result[here] = x
        if here.stop - at == 8:
            strength = strength + x * x
        else:
            rest = node_sum(x * x)
    strength = node_sum(strength)
    if n_classes % 8:
        strength = strength + rest
    strength = jnp.concatenate([strength[:, BLK * r : BLK * (r + 1)] for r in range(8)], axis=0)
    strength = gather(*scatter(strength, strength_out, strength_in, peers_c, cls_send, cls_recv))
    norm = lax.rsqrt(strength + epsilon)
    for r in range(8):
        here = pl.ds(BLK * r, BLK)
        result[:, here] = result[:, here] * norm[r : r + 1]
    for copy in sent:
        copy.wait_send()
    for got, send_sem in scattered:
        pltpu.make_async_copy(got, got, send_sem).wait()


def shards(n_rows, n_cls, seed_scores, block_columns, affinity):
    n_classes, n_nodes = seed_scores.shape
    n_high = n_rows // GROUP
    field = pltpu.VMEM((2048, WIDE), BF16)
    whole = pltpu.VMEM((1024, WIDE), F32)
    turned = pltpu.VMEM((WIDE, 1024), F32)
    code = pltpu.VMEM((24, BLK), F32)
    tile = pltpu.VMEM((8, BLK), F32)
    sums = pltpu.VMEM((16, BLK), F32)
    outside = pltpu.VMEM((4, WIDE, WIDE), F32)
    return pl.pallas_call(
        functools.partial(kernel, n_rows, n_cls),
        out_shape=jax.ShapeDtypeStruct(seed_scores.shape, F32),
        in_specs=[pl.BlockSpec(memory_space=pl.ANY)] * 3,
        out_specs=pl.BlockSpec(memory_space=pltpu.VMEM),
        scratch_shapes=[
            pltpu.SMEM((8, NNZB), jnp.int32),
            pltpu.VMEM((n_classes, n_nodes), F32),
            pltpu.VMEM((8, NNZB, BLK, BLK), BF16),
            pltpu.VMEM((4, WIDE, 10 * BLK), BF16),
            pltpu.VMEM((len(TILES), WIDE, WIDE), BF16),
            field, field, field, field, field,
            whole, whole, whole, whole, whole,
            outside, outside, outside, outside,
            turned, turned,
            code, code, code, tile, tile, tile,
            pltpu.VMEM((4, WIDE, WIDE), BF16), pltpu.VMEM((4, WIDE, WIDE), BF16),
            pltpu.VMEM((2, WIDE, WIDE), BF16), pltpu.VMEM((2, WIDE, WIDE), BF16),
            sums, sums,
            pltpu.VMEM((GROUP - 1, 16, BLK), F32),
            pltpu.VMEM((max(n_high - 1, 1), 16, BLK), F32),
            tile,
            pltpu.VMEM((max(n_cls - 1, 1), 8, BLK), F32),
            pltpu.SemaphoreType.DMA((10,)),
            pltpu.SemaphoreType.DMA((10,)),
            pltpu.SemaphoreType.DMA((10,)),
            pltpu.SemaphoreType.DMA((2,)),
            pltpu.SemaphoreType.DMA((2,)),
            pltpu.SemaphoreType.DMA,
            pltpu.SemaphoreType.DMA,
            pltpu.SemaphoreType.REGULAR((max(n_high // 2 - 1, 1),)),
        ],
        compiler_params=pltpu.CompilerParams(
            collective_id=0, has_side_effects=True, vmem_limit_bytes=VMEM_BYTES
        ),
        cost_estimate=pl.CostEstimate(flops=1600000000, bytes_accessed=4000000, transcendentals=0),
    )(seed_scores, block_columns, affinity)


def solution(mesh):
    return jax.shard_map(
        functools.partial(shards, mesh.shape["rows"], mesh.shape["cls"]),
        mesh=mesh,
        in_specs=(P("cls", "rows"), P("rows", None), P("rows", None, None, None)),
        out_specs=P("cls", "rows"),
        check_vma=False,
    )
```

```python
import functools

import jax
import jax.numpy as jnp
from jax import lax
from jax.experimental import pallas as pl
from jax.experimental.pallas import tpu as pltpu
from jax.sharding import PartitionSpec as P

MESH = pl.DeviceIdType.MESH
BAND = 4
NNZB = 8
BLK = 128
WIDE = 256
GROUP = 8
VMEM_BYTES = 527 * 1024 * 1024 // 10
damping = 0.99
epsilon = 1e-06
F32 = jnp.float32
BF16 = jnp.bfloat16


def column(table, index, width):
    return jnp.broadcast_to(table[:, index : index + 1], (BLK, width))


def node_sum(x):
    return jnp.sum(x, axis=0, keepdims=True)


def ratio(top, bottom):
    good = (bottom > 0) & (top > 0)
    return jnp.where(good, top / jnp.where(good, bottom, 1.0), 0.0)


def combination(early, middle, q):
    g00, g01, g11 = early
    g02, g12, g22 = middle
    g = damping
    gram = [[g00, g01, g02, g12], [g01, g11, g12, g22], [g02, g12, g22, q]]

    def square(p):
        return sum(p[i] * p[j] * gram[i][j] for i in range(len(p)) for j in range(len(p)))

    def energy(p):
        return sum(
            p[i] * p[j] * (gram[i][j] - g * gram[i][j + 1])
            for i in range(len(p))
            for j in range(len(p))
        )

    a0 = ratio(g00, g00 - g * g01)
    r1 = [1.0 - a0, g * a0]
    rr1 = square(r1)
    b0 = ratio(rr1, g00)
    d1 = [r1[0] + b0, r1[1]]
    a1 = ratio(rr1, energy(d1))
    r2 = [r1[0] - a1 * d1[0], r1[1] - a1 * (d1[1] - g * d1[0]), a1 * g * d1[1]]
    rr2 = square(r2)
    b1 = ratio(rr2, rr1)
    d2 = [r2[0] + b1 * d1[0], r2[1] + b1 * d1[1], r2[2]]
    a2 = ratio(rr2, energy(d2))
    return a0 + a1 * d1[0] + a2 * d2[0], a1 * d1[1] + a2 * d2[1], a2 * d2[2]


OWN = {i: (max(i, 2), min(i + 4, 5)) for i in range(4)}
HALO = {0: (0, 1), 1: (1, 1), 2: (6, 6), 3: (6, 7)}
OUTER = (0, 1, 6, 7)
TILES = ((0, 0), (0, 1), (1, 1), (2, 6), (3, 6), (3, 7))


def kernel(
    n_rows, n_cls,
    seed_hbm, columns_hbm, affinity_hbm, result, norm_out,
    columns_ref, seed, raw, band, across, field1, field2a, field2b, field3a, field3b, v0, v1, v2, root, self_part, outer_root, outer_v0, outer_self,
    reach, turned1, turned2,
    code_out, code_left, code_right, apart_out, apart_left, apart_right, first_out, first_in, second_out, second_in,
    part_a, part_b, got_a, got_b, strength_out, strength_in,
    load_sem, halo_send, halo_recv, sum_send, sum_recv, cls_send, cls_recv, relay_sem,
):
    me = lax.axis_index("rows")
    mine = lax.axis_index("cls")
    low, high = lax.rem(me, GROUP), me // GROUP
    n_high = n_rows // GROUP
    total_blocks = n_rows * 8

    columns_copy = pltpu.make_async_copy(columns_hbm, columns_ref, load_sem.at[1])
    columns_copy.start()
    seed_copy = pltpu.make_async_copy(seed_hbm, seed, load_sem.at[2])
    seed_copy.start()
    raw_copy = pltpu.make_async_copy(affinity_hbm, raw, load_sem.at[0])
    raw_copy.start()

    left = {"rows": lax.rem(me + n_rows - 1, n_rows), "cls": mine}
    right = {"rows": lax.rem(me + 1, n_rows), "cls": mine}
    far = sorted(range(1, GROUP), key=lambda d: -min(d, GROUP - d))
    peers_a = [{"rows": high * GROUP + lax.rem(low + d, GROUP), "cls": mine} for d in far]
    peers_b = [{"rows": lax.rem(high + d, n_high) * GROUP + low, "cls": mine} for d in sorted(range(1, n_high), key=lambda d: (d > n_high // 2, -d if d <= n_high // 2 else d))]
    far = sorted(range(1, n_cls), key=lambda d: -min(d, n_cls - d))
    peers_c = [{"rows": me, "cls": lax.rem(mine + d, n_cls)} for d in far]
    barrier = pltpu.get_barrier_semaphore()
    above = {"rows": lax.rem(high + 1, n_high) * GROUP + low, "cls": mine}
    below = {"rows": lax.rem(high + n_high - 1, n_high) * GROUP + low, "cls": mine}
    core = lax.rem(low, 2)
    beside = [
        {"rows": high * GROUP + lax.rem(low + step, GROUP), "cls": mine} for step in (2, GROUP - 2)
    ] + [{"rows": me, "cls": lax.rem(mine + step, n_cls)} for step in (1, n_cls - 1)] + [above, below]
    crossed = [
        {"rows": high * GROUP + lax.rem(low + 1 - 2 * core + step, GROUP), "cls": mine} for step in (GROUP, GROUP + 2, GROUP - 2)
    ]
    partners = [left, right] + beside + crossed
    for device in partners:
        pl.semaphore_signal(barrier, inc=1, device_id=device, device_id_type=MESH)

    sent = []

    def send(source, target, send_sem, recv_sem, device):
        copy = pltpu.make_async_remote_copy(
            src_ref=source, dst_ref=target, send_sem=send_sem, recv_sem=recv_sem,
            device_id=device, device_id_type=MESH,
        )
        copy.start()
        sent.append(copy)
        return copy

    def packed(sums):
        pieces = [half for x in sums for half in (x[:, :BLK], x[:, BLK:])]
        pieces.append(jnp.zeros((16 - len(pieces), BLK), F32))
        return jnp.concatenate(pieces, axis=0)

    def scatter(tile, out, got, peers, send_sem, recv_sem):
        out[...] = tile
        for d, device in enumerate(peers):
            copy = pltpu.make_async_remote_copy(
                src_ref=out, dst_ref=got.at[d], send_sem=send_sem, recv_sem=recv_sem,
                device_id=device, device_id_type=MESH,
            )
            copy.start()
        if peers:
            scattered.append((got, send_sem))
        return tile, got, peers, recv_sem

    def gather(tile, got, peers, recv_sem):
        if peers:
            pltpu.make_async_copy(got, got, recv_sem).wait()
            tile = tile + jnp.sum(got[...], axis=0)
        return tile

    scattered = []

    n_relays = max(n_high // 2 - 1, 1)

    def relay(step):
        if 0 < step <= n_relays:
            pl.semaphore_wait(relay_sem.at[step - 1], len(beside) if step == 1 else 2)
        if step < n_relays:
            for device in beside if step == 0 else (above, below):
                pl.semaphore_signal(relay_sem.at[step], inc=1, device_id=device, device_id_type=MESH)

    lane = lax.broadcasted_iota(jnp.int32, (BLK, BLK), 1)
    diagonal = lane == lax.broadcasted_iota(jnp.int32, (BLK, BLK), 0)
    wide_lane = lax.broadcasted_iota(jnp.int32, (BLK, WIDE), 1).astype(F32)
    columns_copy.wait()
    places = []
    for r in range(8):
        offsets = [
            lax.rem(columns_ref[r, j] - (me * 8 + r) + BAND + total_blocks, total_blocks) for j in range(NNZB)
        ]
        absent = sum(range(9)) - sum(offsets)
        slots = []
        for o in range(9):
            j = 0
            for i in range(1, NNZB):
                j = jnp.where(offsets[i] == o, i, j)
            slots.append((j, (absent != o).astype(F32)))
        places.append(slots)

    seed_copy.wait()
    scores = seed[...]
    class_id = lax.broadcasted_iota(jnp.int32, scores.shape, 0).astype(F32)
    value = node_sum(scores)
    label = node_sum(jnp.where(scores > 0, class_id, 0.0))
    rows = [value[:, BLK * r : BLK * (r + 1)] for r in range(8)]
    rows += [label[:, BLK * r : BLK * (r + 1)] for r in range(8)]
    rows = jnp.concatenate(rows, axis=0)
    code_out[:16] = rows
    code = jnp.concatenate([rows, jnp.zeros((BLK - 16, BLK), F32)], axis=0).T
    for r in range(8):
        v0[BLK * r : BLK * (r + 1)] = jnp.where(
            column(code, 8 + r, WIDE) == wide_lane, column(code, r, WIDE), 0.0
        )

    raw_copy.wait()
    inverses = jnp.zeros((BLK, BLK), F32)
    for r in range(8):
        degree = jnp.sum(jnp.sum(raw[r].astype(F32), axis=0), axis=1, keepdims=True)
        inverse = lax.rsqrt(degree)
        root[BLK * r : BLK * (r + 1)] = jnp.broadcast_to(inverse, (BLK, WIDE))
        inverses = jnp.where(lane == r, inverse, inverses)
    code_out[16:] = inverses.T[:8]

    pl.semaphore_wait(barrier, len(partners))
    to_left = send(code_out, code_right, halo_send.at[0], halo_recv.at[0], left)
    to_right = send(code_out, code_left, halo_send.at[1], halo_recv.at[1], right)
    relay(0)

    def fill(r):
        half = r % 2
        row = pl.ds(BLK * half, BLK)
        apart = None
        for o in range(9):
            slot, present = places[r][o]
            block = raw[r, slot] * present.astype(BF16)
            if o == BAND:
                block = block.astype(F32)
                inverse = root[BLK * r : BLK * (r + 1), :BLK]
                apart = jnp.sum(jnp.where(diagonal, block, 0.0), axis=1, keepdims=True) * inverse * inverse
                self_part[BLK * r : BLK * (r + 1)] = jnp.concatenate([apart, apart], axis=1)
                block = jnp.where(diagonal, 0.0, block).astype(BF16)
            band[r // 2, row, BLK * (o + half) : BLK * (o + half + 1)] = block
        blank = 9 if half == 0 else 0
        band[r // 2, row, BLK * blank : BLK * (blank + 1)] = jnp.zeros((BLK, BLK), BF16)
        return apart

    def part(i, fields, pairs):
        first, last = pairs
        block = band[i, :, WIDE * (first - i) : WIDE * (last + 1 - i)]
        return sum(
            jnp.dot(block, field[WIDE * first : WIDE * (last + 1)], preferred_element_type=F32) for field in fields
        )

    def split(fields, rows, x):
        high = x.astype(BF16)
        fields[0][rows] = high
        fields[1][rows] = (x - high.astype(F32)).astype(BF16)

    field2, field3 = (field2a, field2b), (field3a, field3b)

    def pair(ref, i):
        return ref.at[pl.ds(WIDE * i, WIDE)]

    def own(fields, i):
        return pair(root, i)[...] * part(i, fields, OWN[i])

    def outward(fields, k, pairs=range(4)):
        return sum(
            jnp.dot(across[t], field[WIDE * (i + 2) : WIDE * (i + 3)], preferred_element_type=F32)
            for t, (i, at) in enumerate(TILES)
            if at == k and i in pairs
            for field in fields
        )

    for r in range(8):
        rows = pl.ds(BLK * r, BLK)
        field1[512 + BLK * r : 512 + BLK * (r + 1)] = (root[rows] * v0[rows]).astype(BF16)
    first = {}
    aparts = jnp.zeros((BLK, BLK), F32)
    for i in (0, 3, 1, 2):
        for r in (2 * i, 2 * i + 1):
            aparts = jnp.where(lane == r, fill(r), aparts)
        partial = own((field1,), i)
        first_out[i] = partial.astype(BF16)
        target, device = (first_in.at[2 + i], left) if i < 2 else (first_in.at[i - 2], right)
        first[i] = send(first_out.at[i], target, halo_send.at[2 + i], halo_recv.at[2 + i], device)
        pair(v1, i)[...] = partial + pair(self_part, i)[...] * pair(v0, i)[...]
    apart_out[...] = aparts.T[:8]
    aparts_left = send(apart_out, apart_right, halo_send.at[8], halo_recv.at[8], left)
    aparts_right = send(apart_out, apart_left, halo_send.at[9], halo_recv.at[9], right)
    relay(1)
    for t, (i, k) in enumerate(TILES):
        across[t] = band[i, :, WIDE * (k - i) : WIDE * (k - i + 1)].T
    for h, k in enumerate(OUTER):
        reach[h] = outward((field1,), k)

    to_left.wait_recv()
    to_right.wait_recv()
    outer = jnp.concatenate([code_left[...], code_right[...], jnp.zeros((BLK - 48, BLK), F32)], axis=0).T
    for e in range(4):
        for at, h, base in ((e, e // 2, 4 + e), (12 + e, 2 + e // 2, 24 + e)):
            rows = pl.ds(BLK * (e % 2), BLK)
            here = jnp.where(column(outer, base + 8, WIDE) == wide_lane, column(outer, base, WIDE), 0.0)
            inverse = column(outer, base + 16, WIDE)
            field1[BLK * at : BLK * (at + 1)] = (inverse * here).astype(BF16)
            outer_root[h, rows] = inverse
            outer_v0[h, rows] = here
    for i in range(4):
        inverse = pair(root, i)[...]
        after = pair(v1, i)[...] + inverse * part(i, (field1,), HALO[i])
        pair(v1, i)[...] = after
        field2a[512 + WIDE * i : 512 + WIDE * (i + 1)] = (inverse * after).astype(BF16)

    second = []
    for n, i in enumerate((0, 3)):
        partial = own((field2a,), i)
        second_out[n] = partial.astype(BF16)
        second.append(
            send(second_out.at[n], second_in.at[1 - n], halo_send.at[6 + n], halo_recv.at[6 + n], (left, right)[n])
        )
        pair(v2, i)[...] = partial
    relay(2)
    for i in range(4):
        rows = pl.ds(512 + WIDE * i, WIDE)
        low_part = pair(root, i)[...] * pair(v1, i)[...] - field2a[rows].astype(F32)
        field2b[rows] = low_part.astype(BF16)
    for i in range(4):
        partial = own((field2b,), i) + pair(v2, i)[...] if i in (0, 3) else own(field2, i)
        pair(v2, i)[...] = partial + pair(self_part, i)[...] * pair(v1, i)[...]
    aparts_left.wait_recv()
    aparts_right.wait_recv()
    outer = jnp.concatenate([apart_left[...], apart_right[...], jnp.zeros((BLK - 16, BLK), F32)], axis=0).T
    for e in range(4):
        for h, at in ((e // 2, 4 + e), (2 + e // 2, 8 + e)):
            rows = pl.ds(BLK * (e % 2), BLK)
            apart = column(outer, at, WIDE)
            outer_self[h, rows] = apart
            reach[h, rows] = outer_root[h, rows] * reach[h, rows] + apart * outer_v0[h, rows]
    sums = [node_sum(v0[...] * v0[...]), node_sum(v0[...] * v1[...]), node_sum(v1[...] * v1[...])]
    for i in (3, 2, 0, 1):
        first[i].wait_recv()
    for h, k in enumerate(OUTER):
        after = first_in[h].astype(F32) + reach[h]
        reach[h] = after
        split(field2, pl.ds(WIDE * k, WIDE), outer_root[h] * after)
    late = [jnp.zeros((1, WIDE), F32)] * 3
    for i in range(4):
        inverse = pair(root, i)[...]
        after = pair(v2, i)[...] + inverse * part(i, field2, HALO[i])
        pair(v2, i)[...] = after
        split(field3, pl.ds(512 + WIDE * i, WIDE), inverse * after)
        late[0] = late[0] + node_sum(pair(v0, i)[...] * after)
        late[1] = late[1] + node_sum(pair(v1, i)[...] * after)
        late[2] = late[2] + node_sum(after * after)
    sums += late

    form = jnp.zeros((1, WIDE), F32)
    for i in range(4):
        field = pair(v2, i)[...]
        form = form + node_sum(field * (own(field3, i) + pair(self_part, i)[...] * field))
    for n, (h, k, pairs) in enumerate(((1, 1, (1,)), (2, 6, (2, 3)))):
        inverse = outer_root[h]
        weight = 2.0 * inverse * outward(field3, k, pairs)
        form = form + node_sum(weight * (inverse * outward(field2, k) + outer_self[h] * reach[h]))
        reach[3 * n] = weight
    for n in range(2):
        second[1 - n].wait_recv()
        form = form + node_sum(second_in[n].astype(F32) * reach[3 * n])
    sums.append(form)

    tile = scatter(packed(sums), part_a, got_a, peers_a, sum_send.at[0], sum_recv.at[0])
    for r in range(8):
        turned1[:, BLK * r : BLK * (r + 1)] = v1[BLK * r : BLK * (r + 1)].T
    tile = gather(*tile)
    relay(3)
    tile = scatter(tile, part_b, got_b, peers_b, sum_send.at[1], sum_recv.at[1])
    for r in range(8):
        turned2[:, BLK * r : BLK * (r + 1)] = v2[BLK * r : BLK * (r + 1)].T
    tile = gather(*tile)
    grams = [tile[2 * i : 2 * i + 2] for i in range(7)]
    weights = combination(grams[:3], grams[3:6], grams[6])
    weights = jnp.concatenate(list(weights) + [jnp.zeros((BLK - 6, BLK), F32)], axis=0).T
    n_classes = seed.shape[0]
    columns = [
        jnp.concatenate([weights[:, 2 * i : 2 * i + 1], weights[:, 2 * i + 1 : 2 * i + 2]], axis=0)[:n_classes]
        for i in range(3)
    ]
    n_lanes = seed.shape[1]
    strength = jnp.zeros((8, n_lanes), F32)
    for at in range(0, n_classes, 8):
        here = slice(at, min(at + 8, n_classes))
        c0, c1, c2 = (jnp.broadcast_to(c[here], (here.stop - at, n_lanes)) for c in columns)
        x = c0 * seed[here] + c1 * turned1[here] + c2 * turned2[here]
        result[here] = x
        if here.stop - at == 8:
            strength = strength + x * x
        else:
            rest = node_sum(x * x)
    strength = node_sum(strength)
    if n_classes % 8:
        strength = strength + rest
    strength = jnp.concatenate([strength[:, BLK * r : BLK * (r + 1)] for r in range(8)], axis=0)
    strength = gather(*scatter(strength, strength_out, strength_in, peers_c, cls_send, cls_recv))
    norm = lax.rsqrt(strength + epsilon)
    norm_out[...] = jnp.concatenate([norm[r : r + 1] for r in range(8)], axis=1)
    for copy in sent:
        copy.wait_send()
    for got, send_sem in scattered:
        pltpu.make_async_copy(got, got, send_sem).wait()


def shards(n_rows, n_cls, seed_scores, block_columns, affinity):
    n_classes, n_nodes = seed_scores.shape
    n_high = n_rows // GROUP
    field = pltpu.VMEM((2048, WIDE), BF16)
    whole = pltpu.VMEM((1024, WIDE), F32)
    turned = pltpu.VMEM((WIDE, 1024), F32)
    code = pltpu.VMEM((24, BLK), F32)
    tile = pltpu.VMEM((8, BLK), F32)
    sums = pltpu.VMEM((16, BLK), F32)
    outside = pltpu.VMEM((4, WIDE, WIDE), F32)
    x, norm = pl.pallas_call(
        functools.partial(kernel, n_rows, n_cls),
        out_shape=(jax.ShapeDtypeStruct(seed_scores.shape, F32), jax.ShapeDtypeStruct((1, n_nodes), F32)),
        in_specs=[pl.BlockSpec(memory_space=pl.ANY)] * 3,
        out_specs=(pl.BlockSpec(memory_space=pltpu.VMEM), pl.BlockSpec(memory_space=pltpu.VMEM)),
        scratch_shapes=[
            pltpu.SMEM((8, NNZB), jnp.int32),
            pltpu.VMEM((n_classes, n_nodes), F32),
            pltpu.VMEM((8, NNZB, BLK, BLK), BF16),
            pltpu.VMEM((4, WIDE, 10 * BLK), BF16),
            pltpu.VMEM((len(TILES), WIDE, WIDE), BF16),
            field, field, field, field, field,
            whole, whole, whole, whole, whole,
            outside, outside, outside, outside,
            turned, turned,
            code, code, code, tile, tile, tile,
            pltpu.VMEM((4, WIDE, WIDE), BF16), pltpu.VMEM((4, WIDE, WIDE), BF16),
            pltpu.VMEM((2, WIDE, WIDE), BF16), pltpu.VMEM((2, WIDE, WIDE), BF16),
            sums, sums,
            pltpu.VMEM((GROUP - 1, 16, BLK), F32),
            pltpu.VMEM((max(n_high - 1, 1), 16, BLK), F32),
            tile,
            pltpu.VMEM((max(n_cls - 1, 1), 8, BLK), F32),
            pltpu.SemaphoreType.DMA((3,)),
            pltpu.SemaphoreType.DMA((10,)),
            pltpu.SemaphoreType.DMA((10,)),
            pltpu.SemaphoreType.DMA((2,)),
            pltpu.SemaphoreType.DMA((2,)),
            pltpu.SemaphoreType.DMA,
            pltpu.SemaphoreType.DMA,
            pltpu.SemaphoreType.REGULAR((max(n_high // 2 - 1, 1),)),
        ],
        compiler_params=pltpu.CompilerParams(
            collective_id=0, has_side_effects=True, vmem_limit_bytes=VMEM_BYTES
        ),
        cost_estimate=pl.CostEstimate(flops=1600000000, bytes_accessed=4000000, transcendentals=0),
    )(seed_scores, block_columns, affinity)
    return x * norm


def solution(mesh):
    return jax.shard_map(
        functools.partial(shards, mesh.shape["rows"], mesh.shape["cls"]),
        mesh=mesh,
        in_specs=(P("cls", "rows"), P("rows", None), P("rows", None, None, None)),
        out_specs=P("cls", "rows"),
        check_vma=False,
    )
```

```python
import functools

import jax
import jax.numpy as jnp
from jax import lax
from jax.experimental import pallas as pl
from jax.experimental.pallas import tpu as pltpu
from jax.sharding import PartitionSpec as P

MESH = pl.DeviceIdType.MESH
BAND = 4
NNZB = 8
BLK = 128
WIDE = 256
GROUP = 8
VMEM_BYTES = 527 * 1024 * 1024 // 10
damping = 0.99
epsilon = 1e-06
F32 = jnp.float32
BF16 = jnp.bfloat16


def column(table, index, width):
    return jnp.broadcast_to(table[:, index : index + 1], (BLK, width))


def node_sum(x):
    return jnp.sum(x, axis=0, keepdims=True)


def ratio(top, bottom):
    good = (bottom > 0) & (top > 0)
    return jnp.where(good, top / jnp.where(good, bottom, 1.0), 0.0)


def combination(early, middle, q):
    g00, g01, g11 = early
    g02, g12, g22 = middle
    g = damping
    gram = [[g00, g01, g02, g12], [g01, g11, g12, g22], [g02, g12, g22, q]]

    def square(p):
        return sum(p[i] * p[j] * gram[i][j] for i in range(len(p)) for j in range(len(p)))

    def energy(p):
        return sum(
            p[i] * p[j] * (gram[i][j] - g * gram[i][j + 1])
            for i in range(len(p))
            for j in range(len(p))
        )

    a0 = ratio(g00, g00 - g * g01)
    r1 = [1.0 - a0, g * a0]
    rr1 = square(r1)
    b0 = ratio(rr1, g00)
    d1 = [r1[0] + b0, r1[1]]
    a1 = ratio(rr1, energy(d1))
    r2 = [r1[0] - a1 * d1[0], r1[1] - a1 * (d1[1] - g * d1[0]), a1 * g * d1[1]]
    rr2 = square(r2)
    b1 = ratio(rr2, rr1)
    d2 = [r2[0] + b1 * d1[0], r2[1] + b1 * d1[1], r2[2]]
    a2 = ratio(rr2, energy(d2))
    return a0 + a1 * d1[0] + a2 * d2[0], a1 * d1[1] + a2 * d2[1], a2 * d2[2]


OWN = {i: (max(i, 2), min(i + 4, 5)) for i in range(4)}
HALO = {0: (0, 1), 1: (1, 1), 2: (6, 6), 3: (6, 7)}
OUTER = (0, 1, 6, 7)
TILES = ((0, 0), (0, 1), (1, 1), (2, 6), (3, 6), (3, 7))


def kernel(
    n_rows, n_cls,
    seed_hbm, columns_hbm, affinity_hbm, result, norm_out,
    columns_ref, seed, raw, band, across, field1, field2a, field2b, field3a, field3b, v0, v1, v2, root, self_part, outer_root, outer_v0, outer_self,
    reach, turned1, turned2,
    code_out, code_left, code_right, apart_out, apart_left, apart_right, first_out, first_in, second_out, second_in,
    part_a, part_b, got_a, got_b, strength_out, strength_in,
    load_sem, halo_send, halo_recv, sum_send, sum_recv, cls_send, cls_recv, relay_sem,
):
    me = lax.axis_index("rows")
    mine = lax.axis_index("cls")
    low, high = lax.rem(me, GROUP), me // GROUP
    n_high = n_rows // GROUP
    total_blocks = n_rows * 8

    columns_copy = pltpu.make_async_copy(columns_hbm, columns_ref, load_sem.at[1])
    columns_copy.start()
    seed_copy = pltpu.make_async_copy(seed_hbm, seed, load_sem.at[2])
    seed_copy.start()
    raw_copy = pltpu.make_async_copy(affinity_hbm, raw, load_sem.at[0])
    raw_copy.start()

    left = {"rows": lax.rem(me + n_rows - 1, n_rows), "cls": mine}
    right = {"rows": lax.rem(me + 1, n_rows), "cls": mine}
    far = sorted(range(1, GROUP), key=lambda d: -min(d, GROUP - d))
    peers_a = [{"rows": high * GROUP + lax.rem(low + d, GROUP), "cls": mine} for d in far]
    peers_b = [{"rows": lax.rem(high + d, n_high) * GROUP + low, "cls": mine} for d in sorted(range(1, n_high), key=lambda d: (d > n_high // 2, -d if d <= n_high // 2 else d))]
    far = sorted(range(1, n_cls), key=lambda d: -min(d, n_cls - d))
    peers_c = [{"rows": me, "cls": lax.rem(mine + d, n_cls)} for d in far]
    barrier = pltpu.get_barrier_semaphore()
    above = {"rows": lax.rem(high + 1, n_high) * GROUP + low, "cls": mine}
    below = {"rows": lax.rem(high + n_high - 1, n_high) * GROUP + low, "cls": mine}
    core = lax.rem(low, 2)
    beside = [
        {"rows": high * GROUP + lax.rem(low + step, GROUP), "cls": mine} for step in (2, GROUP - 2)
    ] + [{"rows": me, "cls": lax.rem(mine + step, n_cls)} for step in (1, n_cls - 1)] + [above, below]
    crossed = [
        {"rows": high * GROUP + lax.rem(low + 1 - 2 * core + step, GROUP), "cls": mine} for step in (GROUP, GROUP + 2, GROUP - 2)
    ]
    partners = [left, right] + beside + crossed
    for device in partners:
        pl.semaphore_signal(barrier, inc=1, device_id=device, device_id_type=MESH)

    sent = []

    def send(source, target, send_sem, recv_sem, device):
        copy = pltpu.make_async_remote_copy(
            src_ref=source, dst_ref=target, send_sem=send_sem, recv_sem=recv_sem,
            device_id=device, device_id_type=MESH,
        )
        copy.start()
        sent.append(copy)
        return copy

    def packed(sums):
        pieces = [half for x in sums for half in (x[:, :BLK], x[:, BLK:])]
        pieces.append(jnp.zeros((16 - len(pieces), BLK), F32))
        return jnp.concatenate(pieces, axis=0)

    def scatter(tile, out, got, peers, send_sem, recv_sem):
        out[...] = tile
        for d, device in enumerate(peers):
            copy = pltpu.make_async_remote_copy(
                src_ref=out, dst_ref=got.at[d], send_sem=send_sem, recv_sem=recv_sem,
                device_id=device, device_id_type=MESH,
            )
            copy.start()
        if peers:
            scattered.append((got, send_sem))
        return tile, got, peers, recv_sem

    def gather(tile, got, peers, recv_sem):
        if peers:
            pltpu.make_async_copy(got, got, recv_sem).wait()
            tile = tile + jnp.sum(got[...], axis=0)
        return tile

    scattered = []

    n_relays = max(n_high // 2 - 1, 1)

    def relay(step):
        if 0 < step <= n_relays:
            pl.semaphore_wait(relay_sem.at[step - 1], len(beside) if step == 1 else 2)
        if step < n_relays:
            for device in beside if step == 0 else (above, below):
                pl.semaphore_signal(relay_sem.at[step], inc=1, device_id=device, device_id_type=MESH)

    lane = lax.broadcasted_iota(jnp.int32, (BLK, BLK), 1)
    diagonal = lane == lax.broadcasted_iota(jnp.int32, (BLK, BLK), 0)
    wide_lane = lax.broadcasted_iota(jnp.int32, (BLK, WIDE), 1).astype(F32)
    columns_copy.wait()
    places = []
    for r in range(8):
        offsets = [
            lax.rem(columns_ref[r, j] - (me * 8 + r) + BAND + total_blocks, total_blocks) for j in range(NNZB)
        ]
        absent = sum(range(9)) - sum(offsets)
        slots = []
        for o in range(9):
            j = 0
            for i in range(1, NNZB):
                j = jnp.where(offsets[i] == o, i, j)
            slots.append((j, (absent != o).astype(F32)))
        places.append(slots)

    seed_copy.wait()
    scores = seed[...]
    class_id = lax.broadcasted_iota(jnp.int32, scores.shape, 0).astype(F32)
    value = node_sum(scores)
    label = node_sum(jnp.where(scores > 0, class_id, 0.0))
    rows = [value[:, BLK * r : BLK * (r + 1)] for r in range(8)]
    rows += [label[:, BLK * r : BLK * (r + 1)] for r in range(8)]
    rows = jnp.concatenate(rows, axis=0)
    code_out[:16] = rows
    code = jnp.concatenate([rows, jnp.zeros((BLK - 16, BLK), F32)], axis=0).T
    for r in range(8):
        v0[BLK * r : BLK * (r + 1)] = jnp.where(
            column(code, 8 + r, WIDE) == wide_lane, column(code, r, WIDE), 0.0
        )

    raw_copy.wait()
    inverses = jnp.zeros((BLK, BLK), F32)
    for r in range(8):
        degree = jnp.sum(jnp.sum(raw[r].astype(F32), axis=0), axis=1, keepdims=True)
        inverse = lax.rsqrt(degree)
        root[BLK * r : BLK * (r + 1)] = jnp.broadcast_to(inverse, (BLK, WIDE))
        inverses = jnp.where(lane == r, inverse, inverses)
    code_out[16:] = inverses.T[:8]

    pl.semaphore_wait(barrier, len(partners))
    to_left = send(code_out, code_right, halo_send.at[0], halo_recv.at[0], left)
    to_right = send(code_out, code_left, halo_send.at[1], halo_recv.at[1], right)
    relay(0)

    def fill(r):
        half = r % 2
        row = pl.ds(BLK * half, BLK)
        apart = None
        for o in range(9):
            slot, present = places[r][o]
            block = raw[r, slot] * present.astype(BF16)
            if o == BAND:
                block = block.astype(F32)
                inverse = root[BLK * r : BLK * (r + 1), :BLK]
                apart = jnp.sum(jnp.where(diagonal, block, 0.0), axis=1, keepdims=True) * inverse * inverse
                self_part[BLK * r : BLK * (r + 1)] = jnp.concatenate([apart, apart], axis=1)
                block = jnp.where(diagonal, 0.0, block).astype(BF16)
            band[r // 2, row, BLK * (o + half) : BLK * (o + half + 1)] = block
        blank = 9 if half == 0 else 0
        band[r // 2, row, BLK * blank : BLK * (blank + 1)] = jnp.zeros((BLK, BLK), BF16)
        return apart

    def part(i, fields, pairs):
        first, last = pairs
        block = band[i, :, WIDE * (first - i) : WIDE * (last + 1 - i)]
        return sum(
            jnp.dot(block, field[WIDE * first : WIDE * (last + 1)], preferred_element_type=F32) for field in fields
        )

    def split(fields, rows, x):
        high = x.astype(BF16)
        fields[0][rows] = high
        fields[1][rows] = (x - high.astype(F32)).astype(BF16)

    field2, field3 = (field2a, field2b), (field3a, field3b)

    def pair(ref, i):
        return ref.at[pl.ds(WIDE * i, WIDE)]

    def own(fields, i):
        return pair(root, i)[...] * part(i, fields, OWN[i])

    def outward(fields, k, pairs=range(4)):
        return sum(
            jnp.dot(across[t], field[WIDE * (i + 2) : WIDE * (i + 3)], preferred_element_type=F32)
            for t, (i, at) in enumerate(TILES)
            if at == k and i in pairs
            for field in fields
        )

    for r in range(8):
        rows = pl.ds(BLK * r, BLK)
        field1[512 + BLK * r : 512 + BLK * (r + 1)] = (root[rows] * v0[rows]).astype(BF16)
    first = {}
    aparts = jnp.zeros((BLK, BLK), F32)
    for i in (0, 3, 1, 2):
        for r in (2 * i, 2 * i + 1):
            aparts = jnp.where(lane == r, fill(r), aparts)
        partial = own((field1,), i)
        first_out[i] = partial.astype(BF16)
        target, device = (first_in.at[2 + i], left) if i < 2 else (first_in.at[i - 2], right)
        first[i] = send(first_out.at[i], target, halo_send.at[2 + i], halo_recv.at[2 + i], device)
        pair(v1, i)[...] = partial + pair(self_part, i)[...] * pair(v0, i)[...]
    apart_out[...] = aparts.T[:8]
    aparts_left = send(apart_out, apart_right, halo_send.at[8], halo_recv.at[8], left)
    aparts_right = send(apart_out, apart_left, halo_send.at[9], halo_recv.at[9], right)
    relay(1)
    for t, (i, k) in enumerate(TILES):
        across[t] = band[i, :, WIDE * (k - i) : WIDE * (k - i + 1)].T
    for h, k in enumerate(OUTER):
        reach[h] = outward((field1,), k)

    to_left.wait_recv()
    to_right.wait_recv()
    outer = jnp.concatenate([code_left[...], code_right[...], jnp.zeros((BLK - 48, BLK), F32)], axis=0).T
    for e in range(4):
        for at, h, base in ((e, e // 2, 4 + e), (12 + e, 2 + e // 2, 24 + e)):
            rows = pl.ds(BLK * (e % 2), BLK)
            here = jnp.where(column(outer, base + 8, WIDE) == wide_lane, column(outer, base, WIDE), 0.0)
            inverse = column(outer, base + 16, WIDE)
            field1[BLK * at : BLK * (at + 1)] = (inverse * here).astype(BF16)
            outer_root[h, rows] = inverse
            outer_v0[h, rows] = here
    for i in range(4):
        inverse = pair(root, i)[...]
        after = pair(v1, i)[...] + inverse * part(i, (field1,), HALO[i])
        pair(v1, i)[...] = after
        field2a[512 + WIDE * i : 512 + WIDE * (i + 1)] = (inverse * after).astype(BF16)

    second = []
    for n, i in enumerate((0, 3)):
        partial = own((field2a,), i)
        second_out[n] = partial.astype(BF16)
        second.append(
            send(second_out.at[n], second_in.at[1 - n], halo_send.at[6 + n], halo_recv.at[6 + n], (left, right)[n])
        )
        pair(v2, i)[...] = partial
    relay(2)
    for i in range(4):
        rows = pl.ds(512 + WIDE * i, WIDE)
        low_part = pair(root, i)[...] * pair(v1, i)[...] - field2a[rows].astype(F32)
        field2b[rows] = low_part.astype(BF16)
    for i in range(4):
        partial = own((field2b,), i) + pair(v2, i)[...] if i in (0, 3) else own(field2, i)
        pair(v2, i)[...] = partial + pair(self_part, i)[...] * pair(v1, i)[...]
    aparts_left.wait_recv()
    aparts_right.wait_recv()
    outer = jnp.concatenate([apart_left[...], apart_right[...], jnp.zeros((BLK - 16, BLK), F32)], axis=0).T
    for e in range(4):
        for h, at in ((e // 2, 4 + e), (2 + e // 2, 8 + e)):
            rows = pl.ds(BLK * (e % 2), BLK)
            apart = column(outer, at, WIDE)
            outer_self[h, rows] = apart
            reach[h, rows] = outer_root[h, rows] * reach[h, rows] + apart * outer_v0[h, rows]
    sums = [node_sum(v0[...] * v0[...]), node_sum(v0[...] * v1[...]), node_sum(v1[...] * v1[...])]
    for i in (3, 2, 0, 1):
        first[i].wait_recv()
    for h, k in enumerate(OUTER):
        after = first_in[h].astype(F32) + reach[h]
        reach[h] = after
        split(field2, pl.ds(WIDE * k, WIDE), outer_root[h] * after)
    late = [jnp.zeros((1, WIDE), F32)] * 3
    for i in range(4):
        inverse = pair(root, i)[...]
        after = pair(v2, i)[...] + inverse * part(i, field2, HALO[i])
        pair(v2, i)[...] = after
        split(field3, pl.ds(512 + WIDE * i, WIDE), inverse * after)
        late[0] = late[0] + node_sum(pair(v0, i)[...] * after)
        late[1] = late[1] + node_sum(pair(v1, i)[...] * after)
        late[2] = late[2] + node_sum(after * after)
    sums += late

    form = jnp.zeros((1, WIDE), F32)
    for i in range(4):
        field = pair(v2, i)[...]
        high_part = field3a[512 + WIDE * i : 512 + WIDE * (i + 1)].astype(F32)
        either = 2.0 * pair(root, i)[...] * field - high_part
        form = form + node_sum(either * part(i, (field3a,), OWN[i]) + pair(self_part, i)[...] * field * field)
    for n, (h, k, pairs) in enumerate(((1, 1, (1,)), (2, 6, (2, 3)))):
        inverse = outer_root[h]
        weight = 2.0 * inverse * outward(field3, k, pairs)
        form = form + node_sum(weight * (inverse * outward(field2, k) + outer_self[h] * reach[h]))
        reach[3 * n] = weight
    for n in range(2):
        second[1 - n].wait_recv()
        form = form + node_sum(second_in[n].astype(F32) * reach[3 * n])
    sums.append(form)

    tile = scatter(packed(sums), part_a, got_a, peers_a, sum_send.at[0], sum_recv.at[0])
    for r in range(8):
        turned1[:, BLK * r : BLK * (r + 1)] = v1[BLK * r : BLK * (r + 1)].T
    tile = gather(*tile)
    relay(3)
    tile = scatter(tile, part_b, got_b, peers_b, sum_send.at[1], sum_recv.at[1])
    for r in range(8):
        turned2[:, BLK * r : BLK * (r + 1)] = v2[BLK * r : BLK * (r + 1)].T
    tile = gather(*tile)
    grams = [tile[2 * i : 2 * i + 2] for i in range(7)]
    weights = combination(grams[:3], grams[3:6], grams[6])
    weights = jnp.concatenate(list(weights) + [jnp.zeros((BLK - 6, BLK), F32)], axis=0).T
    n_classes = seed.shape[0]
    columns = [
        jnp.concatenate([weights[:, 2 * i : 2 * i + 1], weights[:, 2 * i + 1 : 2 * i + 2]], axis=0)[:n_classes]
        for i in range(3)
    ]
    n_lanes = seed.shape[1]
    strength = jnp.zeros((8, n_lanes), F32)
    for at in range(0, n_classes, 8):
        here = slice(at, min(at + 8, n_classes))
        c0, c1, c2 = (jnp.broadcast_to(c[here], (here.stop - at, n_lanes)) for c in columns)
        x = c0 * seed[here] + c1 * turned1[here] + c2 * turned2[here]
        result[here] = x
        if here.stop - at == 8:
            strength = strength + x * x
        else:
            rest = node_sum(x * x)
    strength = node_sum(strength)
    if n_classes % 8:
        strength = strength + rest
    strength = jnp.concatenate([strength[:, BLK * r : BLK * (r + 1)] for r in range(8)], axis=0)
    strength = gather(*scatter(strength, strength_out, strength_in, peers_c, cls_send, cls_recv))
    norm = lax.rsqrt(strength + epsilon)
    norm_out[...] = jnp.concatenate([norm[r : r + 1] for r in range(8)], axis=1)
    for copy in sent:
        copy.wait_send()
    for got, send_sem in scattered:
        pltpu.make_async_copy(got, got, send_sem).wait()


def shards(n_rows, n_cls, seed_scores, block_columns, affinity):
    n_classes, n_nodes = seed_scores.shape
    n_high = n_rows // GROUP
    field = pltpu.VMEM((2048, WIDE), BF16)
    whole = pltpu.VMEM((1024, WIDE), F32)
    turned = pltpu.VMEM((WIDE, 1024), F32)
    code = pltpu.VMEM((24, BLK), F32)
    tile = pltpu.VMEM((8, BLK), F32)
    sums = pltpu.VMEM((16, BLK), F32)
    outside = pltpu.VMEM((4, WIDE, WIDE), F32)
    x, norm = pl.pallas_call(
        functools.partial(kernel, n_rows, n_cls),
        out_shape=(jax.ShapeDtypeStruct(seed_scores.shape, F32), jax.ShapeDtypeStruct((1, n_nodes), F32)),
        in_specs=[pl.BlockSpec(memory_space=pl.ANY)] * 3,
        out_specs=(pl.BlockSpec(memory_space=pltpu.VMEM), pl.BlockSpec(memory_space=pltpu.VMEM)),
        scratch_shapes=[
            pltpu.SMEM((8, NNZB), jnp.int32),
            pltpu.VMEM((n_classes, n_nodes), F32),
            pltpu.VMEM((8, NNZB, BLK, BLK), BF16),
            pltpu.VMEM((4, WIDE, 10 * BLK), BF16),
            pltpu.VMEM((len(TILES), WIDE, WIDE), BF16),
            field, field, field, field, field,
            whole, whole, whole, whole, whole,
            outside, outside, outside, outside,
            turned, turned,
            code, code, code, tile, tile, tile,
            pltpu.VMEM((4, WIDE, WIDE), BF16), pltpu.VMEM((4, WIDE, WIDE), BF16),
            pltpu.VMEM((2, WIDE, WIDE), BF16), pltpu.VMEM((2, WIDE, WIDE), BF16),
            sums, sums,
            pltpu.VMEM((GROUP - 1, 16, BLK), F32),
            pltpu.VMEM((max(n_high - 1, 1), 16, BLK), F32),
            tile,
            pltpu.VMEM((max(n_cls - 1, 1), 8, BLK), F32),
            pltpu.SemaphoreType.DMA((3,)),
            pltpu.SemaphoreType.DMA((10,)),
            pltpu.SemaphoreType.DMA((10,)),
            pltpu.SemaphoreType.DMA((2,)),
            pltpu.SemaphoreType.DMA((2,)),
            pltpu.SemaphoreType.DMA,
            pltpu.SemaphoreType.DMA,
            pltpu.SemaphoreType.REGULAR((max(n_high // 2 - 1, 1),)),
        ],
        compiler_params=pltpu.CompilerParams(
            collective_id=0, has_side_effects=True, vmem_limit_bytes=VMEM_BYTES
        ),
        cost_estimate=pl.CostEstimate(flops=1600000000, bytes_accessed=4000000, transcendentals=0),
    )(seed_scores, block_columns, affinity)
    return x * norm


def solution(mesh):
    return jax.shard_map(
        functools.partial(shards, mesh.shape["rows"], mesh.shape["cls"]),
        mesh=mesh,
        in_specs=(P("cls", "rows"), P("rows", None), P("rows", None, None, None)),
        out_specs=P("cls", "rows"),
        check_vma=False,
    )
```

```python
import functools

import jax
import jax.numpy as jnp
from jax import lax
from jax.experimental import pallas as pl
from jax.experimental.pallas import tpu as pltpu
from jax.sharding import PartitionSpec as P

MESH = pl.DeviceIdType.MESH
BAND = 4
NNZB = 8
BLK = 128
WIDE = 256
GROUP = 8
VMEM_BYTES = 527 * 1024 * 1024 // 10
damping = 0.99
epsilon = 1e-06
F32 = jnp.float32
BF16 = jnp.bfloat16


def column(table, index, width):
    return jnp.broadcast_to(table[:, index : index + 1], (BLK, width))


def node_sum(x):
    return jnp.sum(x, axis=0, keepdims=True)


def ratio(top, bottom):
    good = (bottom > 0) & (top > 0)
    return jnp.where(good, top / jnp.where(good, bottom, 1.0), 0.0)


def combination(early, middle, q):
    g00, g01, g11 = early
    g02, g12, g22 = middle
    g = damping
    gram = [[g00, g01, g02, g12], [g01, g11, g12, g22], [g02, g12, g22, q]]

    def square(p):
        return sum(p[i] * p[j] * gram[i][j] for i in range(len(p)) for j in range(len(p)))

    def energy(p):
        return sum(
            p[i] * p[j] * (gram[i][j] - g * gram[i][j + 1])
            for i in range(len(p))
            for j in range(len(p))
        )

    a0 = ratio(g00, g00 - g * g01)
    r1 = [1.0 - a0, g * a0]
    rr1 = square(r1)
    b0 = ratio(rr1, g00)
    d1 = [r1[0] + b0, r1[1]]
    a1 = ratio(rr1, energy(d1))
    r2 = [r1[0] - a1 * d1[0], r1[1] - a1 * (d1[1] - g * d1[0]), a1 * g * d1[1]]
    rr2 = square(r2)
    b1 = ratio(rr2, rr1)
    d2 = [r2[0] + b1 * d1[0], r2[1] + b1 * d1[1], r2[2]]
    a2 = ratio(rr2, energy(d2))
    return a0 + a1 * d1[0] + a2 * d2[0], a1 * d1[1] + a2 * d2[1], a2 * d2[2]


OWN = {i: (max(i, 2), min(i + 4, 5)) for i in range(4)}
HALO = {0: (0, 1), 1: (1, 1), 2: (6, 6), 3: (6, 7)}
OUTER = (0, 1, 6, 7)
TILES = ((0, 0), (0, 1), (1, 1), (2, 6), (3, 6), (3, 7))


def kernel(
    n_rows, n_cls,
    seed_hbm, columns_hbm, affinity_hbm, result, norm_out,
    columns_ref, seed, raw, band, across, field1, field2a, field2b, field3a, field3b, v0, v1, v2, root, self_part, outer_root, outer_v0, outer_self,
    reach, turned1, turned2,
    code_out, code_left, code_right, apart_out, apart_left, apart_right, first_out, first_in, second_out, second_in,
    part_a, part_b, got_a, got_b, strength_out, strength_in,
    load_sem, halo_send, halo_recv, sum_send, sum_recv, cls_send, cls_recv, relay_sem,
):
    me = lax.axis_index("rows")
    mine = lax.axis_index("cls")
    low, high = lax.rem(me, GROUP), me // GROUP
    n_high = n_rows // GROUP
    total_blocks = n_rows * 8

    left = {"rows": lax.rem(me + n_rows - 1, n_rows), "cls": mine}
    right = {"rows": lax.rem(me + 1, n_rows), "cls": mine}
    far = sorted(range(1, GROUP), key=lambda d: -min(d, GROUP - d))
    peers_a = [{"rows": high * GROUP + lax.rem(low + d, GROUP), "cls": mine} for d in far]
    peers_b = [{"rows": lax.rem(high + d, n_high) * GROUP + low, "cls": mine} for d in sorted(range(1, n_high), key=lambda d: (d > n_high // 2, -d if d <= n_high // 2 else d))]
    far = sorted(range(1, n_cls), key=lambda d: -min(d, n_cls - d))
    peers_c = [{"rows": me, "cls": lax.rem(mine + d, n_cls)} for d in far]
    barrier = pltpu.get_barrier_semaphore()
    above = {"rows": lax.rem(high + 1, n_high) * GROUP + low, "cls": mine}
    below = {"rows": lax.rem(high + n_high - 1, n_high) * GROUP + low, "cls": mine}
    core = lax.rem(low, 2)
    beside = [
        {"rows": high * GROUP + lax.rem(low + step, GROUP), "cls": mine} for step in (2, GROUP - 2)
    ] + [{"rows": me, "cls": lax.rem(mine + step, n_cls)} for step in (1, n_cls - 1)] + [above, below]
    crossed = [
        {"rows": high * GROUP + lax.rem(low + 1 - 2 * core + step, GROUP), "cls": mine} for step in (GROUP, GROUP + 2, GROUP - 2)
    ]
    partners = [left, right] + beside + crossed
    for device in partners:
        pl.semaphore_signal(barrier, inc=1, device_id=device, device_id_type=MESH)

    columns_copy = pltpu.make_async_copy(columns_hbm, columns_ref, load_sem.at[1])
    columns_copy.start()
    seed_copy = pltpu.make_async_copy(seed_hbm, seed, load_sem.at[2])
    seed_copy.start()
    raw_copy = pltpu.make_async_copy(affinity_hbm, raw, load_sem.at[0])
    raw_copy.start()

    sent = []

    def send(source, target, send_sem, recv_sem, device):
        copy = pltpu.make_async_remote_copy(
            src_ref=source, dst_ref=target, send_sem=send_sem, recv_sem=recv_sem,
            device_id=device, device_id_type=MESH,
        )
        copy.start()
        sent.append(copy)
        return copy

    def packed(sums):
        pieces = [half for x in sums for half in (x[:, :BLK], x[:, BLK:])]
        pieces.append(jnp.zeros((16 - len(pieces), BLK), F32))
        return jnp.concatenate(pieces, axis=0)

    def scatter(tile, out, got, peers, send_sem, recv_sem):
        out[...] = tile
        for d, device in enumerate(peers):
            copy = pltpu.make_async_remote_copy(
                src_ref=out, dst_ref=got.at[d], send_sem=send_sem, recv_sem=recv_sem,
                device_id=device, device_id_type=MESH,
            )
            copy.start()
        if peers:
            scattered.append((got, send_sem))
        return tile, got, peers, recv_sem

    def gather(tile, got, peers, recv_sem):
        if peers:
            pltpu.make_async_copy(got, got, recv_sem).wait()
            tile = tile + jnp.sum(got[...], axis=0)
        return tile

    scattered = []

    n_relays = max(n_high // 2 - 1, 1)

    def relay(step):
        if 0 < step <= n_relays:
            pl.semaphore_wait(relay_sem.at[step - 1], len(beside) if step == 1 else 2)
        if step < n_relays:
            for device in beside if step == 0 else (above, below):
                pl.semaphore_signal(relay_sem.at[step], inc=1, device_id=device, device_id_type=MESH)

    lane = lax.broadcasted_iota(jnp.int32, (BLK, BLK), 1)
    diagonal = lane == lax.broadcasted_iota(jnp.int32, (BLK, BLK), 0)
    wide_lane = lax.broadcasted_iota(jnp.int32, (BLK, WIDE), 1).astype(F32)
    columns_copy.wait()
    places = []
    for r in range(8):
        offsets = [
            lax.rem(columns_ref[r, j] - (me * 8 + r) + BAND + total_blocks, total_blocks) for j in range(NNZB)
        ]
        absent = sum(range(9)) - sum(offsets)
        slots = []
        for o in range(9):
            j = 0
            for i in range(1, NNZB):
                j = jnp.where(offsets[i] == o, i, j)
            slots.append((j, (absent != o).astype(F32)))
        places.append(slots)

    seed_copy.wait()
    scores = seed[...]
    class_id = lax.broadcasted_iota(jnp.int32, scores.shape, 0).astype(F32)
    value = node_sum(scores)
    label = node_sum(jnp.where(scores > 0, class_id, 0.0))
    rows = [value[:, BLK * r : BLK * (r + 1)] for r in range(8)]
    rows += [label[:, BLK * r : BLK * (r + 1)] for r in range(8)]
    rows = jnp.concatenate(rows, axis=0)
    code_out[:16] = rows
    code = jnp.concatenate([rows, jnp.zeros((BLK - 16, BLK), F32)], axis=0).T
    for r in range(8):
        v0[BLK * r : BLK * (r + 1)] = jnp.where(
            column(code, 8 + r, WIDE) == wide_lane, column(code, r, WIDE), 0.0
        )

    raw_copy.wait()
    inverses = jnp.zeros((BLK, BLK), F32)
    for r in range(8):
        degree = jnp.sum(jnp.sum(raw[r].astype(F32), axis=0), axis=1, keepdims=True)
        inverse = lax.rsqrt(degree)
        root[BLK * r : BLK * (r + 1)] = jnp.broadcast_to(inverse, (BLK, WIDE))
        inverses = jnp.where(lane == r, inverse, inverses)
    code_out[16:] = inverses.T[:8]

    pl.semaphore_wait(barrier, len(partners))
    to_left = send(code_out, code_right, halo_send.at[0], halo_recv.at[0], left)
    to_right = send(code_out, code_left, halo_send.at[1], halo_recv.at[1], right)
    relay(0)

    def fill(r):
        half = r % 2
        row = pl.ds(BLK * half, BLK)
        apart = None
        for o in range(9):
            slot, present = places[r][o]
            block = raw[r, slot] * present.astype(BF16)
            if o == BAND:
                block = block.astype(F32)
                inverse = root[BLK * r : BLK * (r + 1), :BLK]
                apart = jnp.sum(jnp.where(diagonal, block, 0.0), axis=1, keepdims=True) * inverse * inverse
                self_part[BLK * r : BLK * (r + 1)] = jnp.concatenate([apart, apart], axis=1)
                block = jnp.where(diagonal, 0.0, block).astype(BF16)
            band[r // 2, row, BLK * (o + half) : BLK * (o + half + 1)] = block
        blank = 9 if half == 0 else 0
        band[r // 2, row, BLK * blank : BLK * (blank + 1)] = jnp.zeros((BLK, BLK), BF16)
        return apart

    def part(i, fields, pairs):
        first, last = pairs
        block = band[i, :, WIDE * (first - i) : WIDE * (last + 1 - i)]
        return sum(
            jnp.dot(block, field[WIDE * first : WIDE * (last + 1)], preferred_element_type=F32) for field in fields
        )

    def split(fields, rows, x):
        high = x.astype(BF16)
        fields[0][rows] = high
        fields[1][rows] = (x - high.astype(F32)).astype(BF16)

    field2, field3 = (field2a, field2b), (field3a, field3b)

    def pair(ref, i):
        return ref.at[pl.ds(WIDE * i, WIDE)]

    def own(fields, i):
        return pair(root, i)[...] * part(i, fields, OWN[i])

    def outward(fields, k, pairs=range(4)):
        return sum(
            jnp.dot(across[t], field[WIDE * (i + 2) : WIDE * (i + 3)], preferred_element_type=F32)
            for t, (i, at) in enumerate(TILES)
            if at == k and i in pairs
            for field in fields
        )

    for r in range(8):
        rows = pl.ds(BLK * r, BLK)
        field1[512 + BLK * r : 512 + BLK * (r + 1)] = (root[rows] * v0[rows]).astype(BF16)
    first = {}
    aparts = jnp.zeros((BLK, BLK), F32)
    for i in (0, 3, 1, 2):
        for r in (2 * i, 2 * i + 1):
            aparts = jnp.where(lane == r, fill(r), aparts)
        partial = own((field1,), i)
        first_out[i] = partial.astype(BF16)
        target, device = (first_in.at[2 + i], left) if i < 2 else (first_in.at[i - 2], right)
        first[i] = send(first_out.at[i], target, halo_send.at[2 + i], halo_recv.at[2 + i], device)
        pair(v1, i)[...] = partial + pair(self_part, i)[...] * pair(v0, i)[...]
    apart_out[...] = aparts.T[:8]
    aparts_left = send(apart_out, apart_right, halo_send.at[8], halo_recv.at[8], left)
    aparts_right = send(apart_out, apart_left, halo_send.at[9], halo_recv.at[9], right)
    relay(1)
    for t, (i, k) in enumerate(TILES):
        across[t] = band[i, :, WIDE * (k - i) : WIDE * (k - i + 1)].T
    for h, k in enumerate(OUTER):
        reach[h] = outward((field1,), k)

    to_left.wait_recv()
    to_right.wait_recv()
    outer = jnp.concatenate([code_left[...], code_right[...], jnp.zeros((BLK - 48, BLK), F32)], axis=0).T
    for e in range(4):
        for at, h, base in ((e, e // 2, 4 + e), (12 + e, 2 + e // 2, 24 + e)):
            rows = pl.ds(BLK * (e % 2), BLK)
            here = jnp.where(column(outer, base + 8, WIDE) == wide_lane, column(outer, base, WIDE), 0.0)
            inverse = column(outer, base + 16, WIDE)
            field1[BLK * at : BLK * (at + 1)] = (inverse * here).astype(BF16)
            outer_root[h, rows] = inverse
            outer_v0[h, rows] = here
    for i in range(4):
        inverse = pair(root, i)[...]
        after = pair(v1, i)[...] + inverse * part(i, (field1,), HALO[i])
        pair(v1, i)[...] = after
        field2a[512 + WIDE * i : 512 + WIDE * (i + 1)] = (inverse * after).astype(BF16)

    second = []
    for n, i in enumerate((0, 3)):
        partial = own((field2a,), i)
        second_out[n] = partial.astype(BF16)
        second.append(
            send(second_out.at[n], second_in.at[1 - n], halo_send.at[6 + n], halo_recv.at[6 + n], (left, right)[n])
        )
        pair(v2, i)[...] = partial
    relay(2)
    for i in range(4):
        rows = pl.ds(512 + WIDE * i, WIDE)
        low_part = pair(root, i)[...] * pair(v1, i)[...] - field2a[rows].astype(F32)
        field2b[rows] = low_part.astype(BF16)
    for i in range(4):
        partial = own((field2b,), i) + pair(v2, i)[...] if i in (0, 3) else own(field2, i)
        pair(v2, i)[...] = partial + pair(self_part, i)[...] * pair(v1, i)[...]
    aparts_left.wait_recv()
    aparts_right.wait_recv()
    outer = jnp.concatenate([apart_left[...], apart_right[...], jnp.zeros((BLK - 16, BLK), F32)], axis=0).T
    for e in range(4):
        for h, at in ((e // 2, 4 + e), (2 + e // 2, 8 + e)):
            rows = pl.ds(BLK * (e % 2), BLK)
            apart = column(outer, at, WIDE)
            outer_self[h, rows] = apart
            reach[h, rows] = outer_root[h, rows] * reach[h, rows] + apart * outer_v0[h, rows]
    sums = [node_sum(v0[...] * v0[...]), node_sum(v0[...] * v1[...]), node_sum(v1[...] * v1[...])]
    for i in (3, 2, 0, 1):
        first[i].wait_recv()
    for h, k in enumerate(OUTER):
        after = first_in[h].astype(F32) + reach[h]
        reach[h] = after
        split(field2, pl.ds(WIDE * k, WIDE), outer_root[h] * after)
    late = [jnp.zeros((1, WIDE), F32)] * 3
    for i in range(4):
        inverse = pair(root, i)[...]
        after = pair(v2, i)[...] + inverse * part(i, field2, HALO[i])
        pair(v2, i)[...] = after
        split(field3, pl.ds(512 + WIDE * i, WIDE), inverse * after)
        late[0] = late[0] + node_sum(pair(v0, i)[...] * after)
        late[1] = late[1] + node_sum(pair(v1, i)[...] * after)
        late[2] = late[2] + node_sum(after * after)
    sums += late

    form = jnp.zeros((1, WIDE), F32)
    for i in range(4):
        field = pair(v2, i)[...]
        form = form + node_sum(field * (own(field3, i) + pair(self_part, i)[...] * field))
    for n, (h, k, pairs) in enumerate(((1, 1, (1,)), (2, 6, (2, 3)))):
        inverse = outer_root[h]
        weight = 2.0 * inverse * outward(field3, k, pairs)
        form = form + node_sum(weight * (inverse * outward(field2, k) + outer_self[h] * reach[h]))
        reach[3 * n] = weight
    for n in range(2):
        second[1 - n].wait_recv()
        form = form + node_sum(second_in[n].astype(F32) * reach[3 * n])
    sums.append(form)

    tile = scatter(packed(sums), part_a, got_a, peers_a, sum_send.at[0], sum_recv.at[0])
    for r in range(8):
        turned1[:, BLK * r : BLK * (r + 1)] = v1[BLK * r : BLK * (r + 1)].T
    tile = gather(*tile)
    relay(3)
    tile = scatter(tile, part_b, got_b, peers_b, sum_send.at[1], sum_recv.at[1])
    for r in range(8):
        turned2[:, BLK * r : BLK * (r + 1)] = v2[BLK * r : BLK * (r + 1)].T
    tile = gather(*tile)
    grams = [tile[2 * i : 2 * i + 2] for i in range(7)]
    weights = combination(grams[:3], grams[3:6], grams[6])
    weights = jnp.concatenate(list(weights) + [jnp.zeros((BLK - 6, BLK), F32)], axis=0).T
    n_classes = seed.shape[0]
    columns = [
        jnp.concatenate([weights[:, 2 * i : 2 * i + 1], weights[:, 2 * i + 1 : 2 * i + 2]], axis=0)[:n_classes]
        for i in range(3)
    ]
    n_lanes = seed.shape[1]
    strength = jnp.zeros((8, n_lanes), F32)
    for at in range(0, n_classes, 8):
        here = slice(at, min(at + 8, n_classes))
        c0, c1, c2 = (jnp.broadcast_to(c[here], (here.stop - at, n_lanes)) for c in columns)
        x = c0 * seed[here] + c1 * turned1[here] + c2 * turned2[here]
        result[here] = x
        if here.stop - at == 8:
            strength = strength + x * x
        else:
            rest = node_sum(x * x)
    strength = node_sum(strength)
    if n_classes % 8:
        strength = strength + rest
    strength = jnp.concatenate([strength[:, BLK * r : BLK * (r + 1)] for r in range(8)], axis=0)
    strength = gather(*scatter(strength, strength_out, strength_in, peers_c, cls_send, cls_recv))
    norm = lax.rsqrt(strength + epsilon)
    norm_out[...] = jnp.concatenate([norm[r : r + 1] for r in range(8)], axis=1)
    for copy in sent:
        copy.wait_send()
    for got, send_sem in scattered:
        pltpu.make_async_copy(got, got, send_sem).wait()


def shards(n_rows, n_cls, seed_scores, block_columns, affinity):
    n_classes, n_nodes = seed_scores.shape
    n_high = n_rows // GROUP
    field = pltpu.VMEM((2048, WIDE), BF16)
    whole = pltpu.VMEM((1024, WIDE), F32)
    turned = pltpu.VMEM((WIDE, 1024), F32)
    code = pltpu.VMEM((24, BLK), F32)
    tile = pltpu.VMEM((8, BLK), F32)
    sums = pltpu.VMEM((16, BLK), F32)
    outside = pltpu.VMEM((4, WIDE, WIDE), F32)
    x, norm = pl.pallas_call(
        functools.partial(kernel, n_rows, n_cls),
        out_shape=(jax.ShapeDtypeStruct(seed_scores.shape, F32), jax.ShapeDtypeStruct((1, n_nodes), F32)),
        in_specs=[pl.BlockSpec(memory_space=pl.ANY)] * 3,
        out_specs=(pl.BlockSpec(memory_space=pltpu.VMEM), pl.BlockSpec(memory_space=pltpu.VMEM)),
        scratch_shapes=[
            pltpu.SMEM((8, NNZB), jnp.int32),
            pltpu.VMEM((n_classes, n_nodes), F32),
            pltpu.VMEM((8, NNZB, BLK, BLK), BF16),
            pltpu.VMEM((4, WIDE, 10 * BLK), BF16),
            pltpu.VMEM((len(TILES), WIDE, WIDE), BF16),
            field, field, field, field, field,
            whole, whole, whole, whole, whole,
            outside, outside, outside, outside,
            turned, turned,
            code, code, code, tile, tile, tile,
            pltpu.VMEM((4, WIDE, WIDE), BF16), pltpu.VMEM((4, WIDE, WIDE), BF16),
            pltpu.VMEM((2, WIDE, WIDE), BF16), pltpu.VMEM((2, WIDE, WIDE), BF16),
            sums, sums,
            pltpu.VMEM((GROUP - 1, 16, BLK), F32),
            pltpu.VMEM((max(n_high - 1, 1), 16, BLK), F32),
            tile,
            pltpu.VMEM((max(n_cls - 1, 1), 8, BLK), F32),
            pltpu.SemaphoreType.DMA((3,)),
            pltpu.SemaphoreType.DMA((10,)),
            pltpu.SemaphoreType.DMA((10,)),
            pltpu.SemaphoreType.DMA((2,)),
            pltpu.SemaphoreType.DMA((2,)),
            pltpu.SemaphoreType.DMA,
            pltpu.SemaphoreType.DMA,
            pltpu.SemaphoreType.REGULAR((max(n_high // 2 - 1, 1),)),
        ],
        compiler_params=pltpu.CompilerParams(
            collective_id=0, has_side_effects=True, vmem_limit_bytes=VMEM_BYTES
        ),
        cost_estimate=pl.CostEstimate(flops=1600000000, bytes_accessed=4000000, transcendentals=0),
    )(seed_scores, block_columns, affinity)
    return x * norm


def solution(mesh):
    return jax.shard_map(
        functools.partial(shards, mesh.shape["rows"], mesh.shape["cls"]),
        mesh=mesh,
        in_specs=(P("cls", "rows"), P("rows", None), P("rows", None, None, None)),
        out_specs=P("cls", "rows"),
        check_vma=False,
    )
```
